512 devices in a mesh: ctx: 64 (over y, x, core), tp: 8 (over z).
Axes of the slice: x: 4, y: 8, z: 8, core: 2. Of those that a mesh axis runs over, the one named last changes fastest.
Arguments:
- query_act: bfloat16 [16384, 4096], P('ctx', 'tp'), may hold values from -6 to 6
- key_act: bfloat16 [16384, 4096], P('ctx', 'tp'), may hold values from -6 to 6
- value_act: bfloat16 [16384, 4096], P('ctx', 'tp'), may hold values from -6 to 6
- grad_gated: bfloat16 [16384, 4096], P('ctx', 'tp'), may hold values from -18 to 18
- filter_taps: float32 [128, 256], P('ctx', 'tp'), may hold values from -0.5 to 0.5
- decay_rate: float32 [256], P('tp'), may hold values from 0.002 to 0.03
Outputs:
- grad_query: bfloat16 [16384, 4096], P('ctx', 'tp')
- grad_key: bfloat16 [16384, 4096], P('ctx', 'tp')
- grad_value: bfloat16 [16384, 4096], P('ctx', 'tp')
- grad_filter: float32 [128, 256], P('ctx', 'tp')
The draws below stay inside these ranges and needn't reach their ends.
All inputs are finite; a program needn't handle non-finite values.
Results may differ from the reference program's by a relative error of at most 0.001.
Values may be sent and summed in bfloat16 or wider, within the bound.
A program may use at most 64 MiB of HBM per device.

```python
import math
import jax
import jax.numpy as jnp
from jax import lax

D = 4096
G = 256
L = 128
TOKENS = 16384


def draw_grad_gated(key, part):
    key = jax.random.fold_in(key, 7)
    scale_key = jax.random.fold_in(key, 0)
    noise_key = jax.random.fold_in(key, 2)
    channel_scale = jnp.exp(jax.random.uniform(scale_key, (1, D), jnp.float32, math.log(0.3), math.log(3.0)))
    values = channel_scale * jnp.clip(jax.random.normal(noise_key, (TOKENS, D), jnp.float32), -6.0, 6.0)
    return values.astype(jnp.bfloat16)


def block_levels(rng, shape, pieces, smallest, largest):
    loudness = 1.0
    for position, parts in pieces:
        heights = jax.random.uniform(jax.random.fold_in(jax.random.fold_in(rng, 6), position), (parts,), jnp.float32, smallest / len(pieces), largest / len(pieces))
        loudness = loudness * jnp.repeat(jnp.exp(heights), shape[position] // parts).reshape((-1,) + (1,) * (len(shape) - 1 - position))
    return loudness


def scatter_about(stream_key, shape, spread, reach, pieces=(), held_as=jnp.bfloat16):
    gain = block_levels(stream_key, shape, pieces, -0.22, 0.18) if pieces else 1.0
    drawn = jax.random.normal(stream_key, shape, jnp.float32) * spread * gain
    return jnp.minimum(jnp.maximum(drawn, -reach), reach).astype(held_as)


def setup_inputs(seed: int = 0) -> dict:
    splits = jax.random.split(jax.random.key(seed), 7)
    query_act = scatter_about(splits[0], (TOKENS, D), 1.0, 6.0, ((0, 64), (1, 8)))
    key_act = scatter_about(splits[1], (TOKENS, D), 1.0, 6.0, ((0, 64), (1, 8)))
    value_act = scatter_about(splits[2], (TOKENS, D), 1.0, 6.0, ((0, 64), (1, 8)))
    grad_gated = draw_grad_gated(jax.random.fold_in(splits[6], 71), 0)
    filter_taps = scatter_about(splits[4], (L, G), L ** -0.5, 0.5, ((0, 64), (1, 8)), jnp.float32)
    decay_rate = jnp.clip(jnp.exp(math.log(0.03) - 2.70805 * jax.random.uniform(splits[5], (G,), jnp.float32) ** block_levels(splits[5], (G,), ((0, 8),), -0.2, 0.2)), 0.002, 0.03)
    return {"query_act": query_act, "key_act": key_act, "value_act": value_act, "grad_gated": grad_gated, "filter_taps": filter_taps, "decay_rate": decay_rate}


def reference(query_act, key_act, value_act, grad_gated, filter_taps, decay_rate):
    tap_index = jnp.arange(L, dtype=jnp.float32)[:, None]
    damping = jnp.exp(-decay_rate[None, :] * tap_index)
    taps = filter_taps * damping
    per_group = D // G
    channel_taps = jnp.repeat(taps, per_group, axis=1)
    products = key_act.astype(jnp.float32) * value_act.astype(jnp.float32)
    slopes = grad_gated.astype(jnp.float32) * query_act.astype(jnp.float32)
    padded_products = jnp.concatenate([jnp.zeros((L, D), jnp.float32), products], axis=0)
    padded_slopes = jnp.concatenate([slopes, jnp.zeros((L, D), jnp.float32)], axis=0)

    def forward_tap(index, total):
        start = (L - index).astype(jnp.int32)
        piece = lax.dynamic_slice_in_dim(padded_products, start, TOKENS, 0)
        weight = lax.dynamic_slice_in_dim(channel_taps, index.astype(jnp.int32), 1, 0)
        return total + weight * piece

    def backward_tap(index, total):
        piece = lax.dynamic_slice_in_dim(padded_slopes, index.astype(jnp.int32), TOKENS, 0)
        weight = lax.dynamic_slice_in_dim(channel_taps, index.astype(jnp.int32), 1, 0)
        return total + weight * piece

    mixed = lax.fori_loop(0, L, forward_tap, jnp.zeros((TOKENS, D), jnp.float32))
    back = lax.fori_loop(0, L, backward_tap, jnp.zeros((TOKENS, D), jnp.float32))
    grad_query = (grad_gated.astype(jnp.float32) * mixed).astype(jnp.bfloat16)
    grad_key = (back * value_act.astype(jnp.float32)).astype(jnp.bfloat16)
    grad_value = (back * key_act.astype(jnp.float32)).astype(jnp.bfloat16)

    def tap_gradient(index):
        start = (L - index).astype(jnp.int32)
        piece = lax.dynamic_slice_in_dim(padded_products, start, TOKENS, 0)
        column = jnp.sum(slopes * piece, axis=0)
        return jnp.sum(column.reshape(G, per_group), axis=1)

    lagged = lax.map(tap_gradient, jnp.arange(L, dtype=jnp.int32))
    grad_filter = lagged * damping / float(TOKENS)
    return (grad_query, grad_key, grad_value, grad_filter)
```

```python
import functools

import jax
import jax.numpy as jnp
from jax import lax
from jax.experimental import pallas as pl
from jax.experimental.pallas import tpu as pltpu
from jax.sharding import PartitionSpec as P

L = 128
CH = 16
LANES = 128
CHUNKS = 4
GROUPS = LANES // CH
MESH = pl.DeviceIdType.MESH
F32, BF16 = jnp.float32, jnp.bfloat16


def dot(a, b, dims):
    return lax.dot_general(a, b, (dims, ((), ())), preferred_element_type=F32)


def split_product(a, b):
    whole = jnp.transpose(a.astype(F32) * b.astype(F32))
    high = whole.astype(BF16)
    return high, (whole - high.astype(F32)).astype(BF16)


def prepare(c, k, v, g, q, pt, st):
    for (a, b, out, first) in ((k, v, pt, L), (g, q, st, 0)):
        high, low = split_product(a[c], b[c])
        out[c, 0, :, first : first + 2 * L] = high
        out[c, 1, :, first : first + 2 * L] = low


def prepare_halo(c, halo, out, first, here):
    high, low = split_product(halo[c, 0], halo[c, 1])
    keep = jnp.where(here, 1.0, 0.0).astype(BF16)
    out[c, 0, :, first : first + L] = high * keep
    out[c, 1, :, first : first + L] = low * keep


def lag_inner(c, pt, st, diag):
    row = lax.broadcasted_iota(jnp.int32, (L, L), 0)
    lane = lax.broadcasted_iota(jnp.int32, (L, L), 1)
    upper = lane >= row
    none = jnp.zeros((CH, L), BF16)
    for r in range(GROUPS):
        rows = slice(CH * r, CH * r + CH)
        p = [[pt[c, part, rows, L * b : L * b + L] for b in (1, 2)] for part in (0, 1)]
        s = [[st[c, part, rows, L * b : L * b + L] for b in (0, 1)] for part in (0, 1)]
        left = jnp.concatenate([p[0][0], p[0][1], p[1][0], p[1][1], p[0][0], p[0][1]], axis=0)
        right = jnp.concatenate(
            [
                jnp.concatenate([s[part][0], s[part][1]], axis=1) if b == 0 else jnp.concatenate([s[part][1], none], axis=1)
                for part in (0, 0, 1)
                for b in (0, 1)
            ],
            axis=0,
        )
        both = dot(left, right, ((0,), (0,)))
        diag[c, r] = jnp.where(upper, both[:, :L], both[:, L:])


def lag_cross(c, pt, st, pb, sb, diag, folded, lag):
    row = lax.broadcasted_iota(jnp.int32, (L, L), 0)
    lane = lax.broadcasted_iota(jnp.int32, (L, L), 1)
    upper = lane >= row
    none = jnp.zeros((CH, L), BF16)
    for r in range(0, GROUPS, 2):
        left, right = [], []
        for e in range(2):
            rows = slice(CH * (r + e), CH * (r + e) + CH)
            p = [pt[c, part, rows, pl.ds(pl.multiple_of(pb * L, L), L)] for part in (0, 1)]
            s = [st[c, part, rows, pl.ds(pl.multiple_of(sb * L, L), L)] for part in (0, 1)]
            for i, j in ((0, 0), (1, 0), (0, 1)):
                left.append(p[i])
                right.append(jnp.concatenate([s[j], none] if e == 0 else [none, s[j]], axis=1))
        both = dot(jnp.concatenate(left, axis=0), jnp.concatenate(right, axis=0), ((0,), (0,)))
        for e in range(2):
            whole = diag[c, r + e] + jnp.where(upper, 0.0, both[:, L * e : L * e + L])
            total = whole[:8]
            for a in range(8, L, 8):
                total = total + pltpu.roll(whole[a : a + 8], L - a, 1)
            folded[8 * (r + e) : 8 * (r + e) + 8, :] = total
    total = folded[pl.ds(0, GROUPS, stride=8), :]
    for a in range(1, 8):
        total = total + pltpu.roll(folded[pl.ds(a, GROUPS, stride=8), :], L - a, 1)
    lag[c] = total


def toeplitz(c, taps, band):
    row = lax.broadcasted_iota(jnp.int32, (L, L), 0)
    lane = lax.broadcasted_iota(jnp.int32, (L, L), 1)
    upper = jnp.where(lane >= row, 1.0, 0.0).astype(BF16)
    for r in range(GROUPS):
        line = taps[c, r : r + 1, :]
        whole = pltpu.roll(jnp.broadcast_to(line, (L, L)), 0, 1, stride=1, stride_axis=0)
        high = whole.astype(BF16)
        low = (whole - high.astype(F32)).astype(BF16)
        for i, part in ((0, high), (1, low)):
            now = part * upper
            band[c, r, L:, L * i : L * i + L] = now
            band[c, r, :L, L * i : L * i + L] = part - now


def convolve(c, pt, st, band, mixed, back):
    for r in range(GROUPS):
        rows = slice(CH * r, CH * r + CH)
        w = band[c, r]
        w_back = jnp.concatenate(
            [
                jnp.concatenate([w[L:, :L], w[:L, :L]], axis=1),
                jnp.concatenate([w[L:, L:], w[:L, L:]], axis=1),
            ],
            axis=0,
        )
        for x, weights, dims, out in ((pt, w, ((1,), (0,)), mixed), (st, w_back, ((1,), (1,)), back)):
            left = jnp.concatenate(
                [x[c, part, rows, L * b : L * b + 2 * L] for part in (0, 1) for b in (0, 1)], axis=0
            )
            got = dot(left, weights, dims)
            for b in (0, 1):
                out[rows, L * b : L * b + L] = (
                    got[CH * b : CH * b + CH, :L]
                    + got[CH * b : CH * b + CH, L:]
                    + got[CH * (2 + b) : CH * (2 + b) + CH, :L]
                )


def finish(c, k, v, g, mixed, back, out):
    forward = jnp.transpose(mixed[...])
    backward = jnp.transpose(back[...])
    out[0, c] = (g[c].astype(F32) * forward).astype(BF16)
    out[1, c] = (backward * v[c].astype(F32)).astype(BF16)
    out[2, c] = (backward * k[c].astype(F32)).astype(BF16)


def kernel(
    ny, nx, rows_here,
    k_hbm, v_hbm, q_hbm, g_hbm, taps_in, decay_in,
    gq_hbm, gk_hbm, gv_hbm, gf_out,
    k, v, q, g, kv_halo, qg_halo, pt, st, band, diag, folded, taps, lag, mixed, back, out,
    mine, gather_x, gather_y, partial, reduce_y, reduce_mine, reduce_x, final, summed,
    in_sem, out_sem, kv_send, kv_recv, qg_send, qg_recv,
    gx_send, gx_recv, gy_send, gy_recv, ry_send, ry_recv, rx_send, rx_recv,
):
    n = ny * nx
    me = lax.axis_index("ctx")
    y, xc = me // nx, me % nx
    core = me % 2
    nxt, prv = (me + 1) % n, (me + n - 1) % n
    tokens = 2 * L

    def at_x(d):
        return y * nx + (xc + d) % nx

    def at_y(d):
        return ((y + d) % ny) * nx + xc

    def lanes(c):
        return pl.ds(pl.multiple_of(c * LANES, LANES), LANES)

    def loads(c):
        return [
            pltpu.make_async_copy(src.at[:, lanes(c)], dst.at[c], in_sem.at[i, c])
            for i, (src, dst) in enumerate(((k_hbm, k), (v_hbm, v), (g_hbm, g), (q_hbm, q)))
        ]

    def stores(c):
        return [
            pltpu.make_async_copy(out.at[i, c], dst.at[:, lanes(c)], out_sem.at[i, c])
            for i, dst in enumerate((gq_hbm, gk_hbm, gv_hbm))
        ]

    def kv_copies(c):
        return [
            pltpu.make_async_remote_copy(
                src_ref=src.at[tokens - L :, lanes(c)], dst_ref=kv_halo.at[c, i],
                send_sem=kv_send.at[c, i], recv_sem=kv_recv.at[c, i],
                device_id={"ctx": nxt}, device_id_type=MESH,
            )
            for i, src in enumerate((k_hbm, v_hbm))
        ]

    def qg_copies(c):
        return [
            pltpu.make_async_remote_copy(
                src_ref=src.at[:L, lanes(c)], dst_ref=qg_halo.at[c, i],
                send_sem=qg_send.at[c, i], recv_sem=qg_recv.at[c, i],
                device_id={"ctx": prv}, device_id_type=MESH,
            )
            for i, src in enumerate((g_hbm, q_hbm))
        ]

    def exchange(src, dst, slot, there, send, recv, d):
        return pltpu.make_async_remote_copy(
            src_ref=src, dst_ref=dst.at[slot], send_sem=send.at[d - 1], recv_sem=recv.at[d - 1],
            device_id={"ctx": there}, device_id_type=MESH,
        )

    def gx_copy(d):
        return exchange(mine, gather_x, xc, at_x(d), gx_send, gx_recv, d)

    def gy_copy(d):
        return exchange(reduce_mine, gather_y, y, at_y(d), gy_send, gy_recv, d)

    def ry_copy(d):
        return exchange(partial.at[(y + d) % ny], reduce_y, y, at_y(d), ry_send, ry_recv, d)

    def rx_copy(d):
        return exchange(final, reduce_x, xc, at_x(d), rx_send, rx_recv, d)

    def each(copy, count, act):
        def step(d, carry):
            act(copy(d))
            return carry

        lax.fori_loop(1, count, step, 0)

    for i in range(CHUNKS):
        for copy in loads(i):
            copy.start()

    barrier = pltpu.get_barrier_semaphore()

    def greet(there):
        pl.semaphore_signal(barrier, inc=1, device_id={"ctx": there}, device_id_type=MESH)

    greet(nxt)
    greet(prv)
    each(at_x, nx, greet)
    each(at_y, ny, greet)

    block = nx * rows_here
    row = lax.broadcasted_iota(jnp.int32, (block, L), 0)
    groups = taps_in.shape[1]
    whole = jnp.zeros((block, L), F32)
    for i in range(rows_here):
        line = jnp.concatenate([taps_in[i : i + 1, :], jnp.zeros((1, L - groups), F32)], axis=1)
        whole = jnp.where(row == xc * rows_here + i, line, whole)
    mine[...] = whole
    gather_x[pl.ds(xc, 1)] = whole[None]

    pl.semaphore_wait(barrier, 2 + (nx - 1) + (ny - 1))
    each(gx_copy, nx, lambda copy: copy.start())
    for i in range(CHUNKS):
        for copy in kv_copies(i):
            copy.start()
        for copy in qg_copies((i + 2) % CHUNKS):
            copy.start()

    def prepare_step(c, carry):
        for copy in loads(c):
            copy.wait()
        prepare(c, k, v, g, q, pt, st)
        lag_inner(c, pt, st, diag)
        return carry

    lax.fori_loop(0, 2, prepare_step, 0)
    each(gx_copy, nx, lambda copy: copy.wait_recv())
    total = gather_x[0]
    for i in range(1, nx):
        total = total + gather_x[i]
    reduce_mine[...] = total
    gather_y[pl.ds(y, 1)] = total[None]
    each(gy_copy, ny, lambda copy: copy.start())
    lax.fori_loop(2, CHUNKS, prepare_step, 0)

    each(gy_copy, ny, lambda copy: copy.wait_recv())
    decay = decay_in[...]
    decay = jnp.concatenate([decay, jnp.zeros((1, L - groups), F32)], axis=1)
    step = lax.broadcasted_iota(jnp.int32, (L, L), 0).astype(F32)
    all_taps = gather_y[...].reshape(L, L) * jnp.exp(-decay * step)
    turned = jnp.transpose(all_taps)
    for c in range(CHUNKS):
        taps[c] = turned[GROUPS * c : GROUPS * c + GROUPS]

    def toeplitz_step(c, carry):
        toeplitz(c, taps, band)
        return carry

    lax.fori_loop(0, CHUNKS, toeplitz_step, 0)

    def kv_step(c, carry):
        for copy in kv_copies(c):
            copy.wait_recv()
        prepare_halo(c, kv_halo, pt, 0, me > 0)
        return carry

    def qg_step(c, carry):
        for copy in qg_copies(c):
            copy.wait_recv()
        prepare_halo(c, qg_halo, st, 2 * L, me < n - 1)
        return carry

    def cross_step(i, carry):
        c = (i + 2 - 2 * core) % CHUNKS

        @pl.when(c < 2)
        def _():
            kv_step(c, 0)

        @pl.when(c >= 2)
        def _():
            qg_step(c, 0)

        late = c // 2
        lag_cross(c, pt, st, 2 * late, 2 * late, diag, folded, lag)
        return carry

    lax.fori_loop(0, CHUNKS, cross_step, 0)

    per_lag = jnp.transpose(
        jnp.concatenate([lag[c] for c in range(CHUNKS)] + [jnp.zeros((L - CHUNKS * GROUPS, L), F32)], axis=0)
    )
    partial[...] = per_lag.reshape(ny, block, L)
    reduce_y[pl.ds(y, 1)] = partial[pl.ds(y, 1)]
    each(ry_copy, ny, lambda copy: copy.start())

    def output_step(i, carry):
        c = (i + 2 * core) % CHUNKS

        @pl.when(c < 2)
        def _():
            qg_step(c, 0)

        @pl.when(c >= 2)
        def _():
            kv_step(c, 0)

        convolve(c, pt, st, band, mixed, back)
        finish(c, k, v, g, mixed, back, out)
        for copy in stores(c):
            copy.start()
        return carry

    lax.fori_loop(0, 2, output_step, 0)
    each(ry_copy, ny, lambda copy: copy.wait_recv())
    total = reduce_y[0]
    for i in range(1, ny):
        total = total + reduce_y[i]
    final[...] = total
    reduce_x[pl.ds(xc, 1)] = total[None]
    each(rx_copy, nx, lambda copy: copy.start())
    lax.fori_loop(2, CHUNKS, output_step, 0)

    each(rx_copy, nx, lambda copy: copy.wait_recv())
    total = reduce_x[0]
    for i in range(1, nx):
        total = total + reduce_x[i]
    summed[...] = total
    lag_index = (me * rows_here + lax.broadcasted_iota(jnp.int32, (rows_here, L), 0)).astype(F32)
    share = summed[pl.ds(xc * rows_here, rows_here), :] * jnp.exp(-decay * lag_index) / float(tokens * n)
    gf_out[...] = share[:, :groups]

    for i in range(CHUNKS):
        for copy in stores(i):
            copy.wait()
        for copy in kv_copies(i):
            copy.wait_send()
        for copy in qg_copies(i):
            copy.wait_send()
    each(gx_copy, nx, lambda copy: copy.wait_send())
    each(gy_copy, ny, lambda copy: copy.wait_send())
    each(ry_copy, ny, lambda copy: copy.wait_send())
    each(rx_copy, nx, lambda copy: copy.wait_send())


def on_device(ny, nx, query_act, key_act, value_act, grad_gated, filter_taps, decay_rate):
    tokens, channels = query_act.shape
    rows_here, groups = filter_taps.shape
    block = nx * rows_here
    whole = jax.ShapeDtypeStruct((tokens, channels), BF16)
    vmem = pl.BlockSpec(memory_space=pltpu.VMEM)
    hbm = pl.BlockSpec(memory_space=pl.ANY)
    dma = pltpu.SemaphoreType.DMA
    chunked = pltpu.VMEM((CHUNKS, tokens, LANES), BF16)
    halo = pltpu.VMEM((CHUNKS, 2, L, LANES), BF16)
    wide = pltpu.VMEM((CHUNKS, 2, LANES, 3 * L), BF16)
    return pl.pallas_call(
        functools.partial(kernel, ny, nx, rows_here),
        out_shape=(whole, whole, whole, jax.ShapeDtypeStruct((rows_here, groups), F32)),
        in_specs=[hbm] * 4 + [vmem] * 2,
        out_specs=(hbm, hbm, hbm, vmem),
        scratch_shapes=[
            chunked, chunked, chunked, chunked, halo, halo, wide, wide,
            pltpu.VMEM((CHUNKS, GROUPS, 2 * L, 2 * L), BF16),
            pltpu.VMEM((CHUNKS, GROUPS, L, L), F32),
            pltpu.VMEM((8 * GROUPS, L), F32),
            pltpu.VMEM((CHUNKS, GROUPS, L), F32),
            pltpu.VMEM((CHUNKS, GROUPS, L), F32),
            pltpu.VMEM((LANES, tokens), F32),
            pltpu.VMEM((LANES, tokens), F32),
            pltpu.VMEM((3, CHUNKS, tokens, LANES), BF16),
            pltpu.VMEM((block, L), F32),
            pltpu.VMEM((nx, block, L), F32),
            pltpu.VMEM((ny, block, L), F32),
            pltpu.VMEM((ny, block, L), F32),
            pltpu.VMEM((ny, block, L), F32),
            pltpu.VMEM((block, L), F32),
            pltpu.VMEM((nx, block, L), F32),
            pltpu.VMEM((block, L), F32),
            pltpu.VMEM((block, L), F32),
            dma((4, CHUNKS)), dma((3, CHUNKS)),
            dma((CHUNKS, 2)), dma((CHUNKS, 2)), dma((CHUNKS, 2)), dma((CHUNKS, 2)),
            dma((nx - 1,)), dma((nx - 1,)), dma((ny - 1,)), dma((ny - 1,)),
            dma((ny - 1,)), dma((ny - 1,)), dma((nx - 1,)), dma((nx - 1,)),
        ],
        compiler_params=pltpu.CompilerParams(
            collective_id=0, has_side_effects=True, vmem_limit_bytes=60 * 1024 * 1024
        ),
    )(key_act, value_act, query_act, grad_gated, filter_taps, decay_rate.reshape(1, groups))


def solution(mesh):
    n = mesh.shape["ctx"]
    nx = 8 if n >= 64 else 4
    return jax.shard_map(
        functools.partial(on_device, n // nx, nx),
        mesh=mesh,
        in_specs=(P("ctx", "tp"),) * 5 + (P("tp"),),
        out_specs=(P("ctx", "tp"),) * 4,
        check_vma=False,
    )
```

```python
import functools

import jax
import jax.numpy as jnp
from jax import lax
from jax.experimental import pallas as pl
from jax.experimental.pallas import tpu as pltpu
from jax.sharding import PartitionSpec as P

L = 128
CH = 16
LANES = 128
CHUNKS = 4
GROUPS = LANES // CH
VMEM_LIMIT = 53 * 1024 * 1024
MESH = pl.DeviceIdType.MESH
F32, BF16 = jnp.float32, jnp.bfloat16


def dot(a, b, dims):
    return lax.dot_general(a, b, (dims, ((), ())), preferred_element_type=F32)


def split_product(a, b):
    whole = jnp.transpose(a.astype(F32) * b.astype(F32))
    high = whole.astype(BF16)
    return high, (whole - high.astype(F32)).astype(BF16)


def lanes(c):
    return pl.ds(pl.multiple_of(c * LANES, LANES), LANES)


def prepare(c, k, v, g, q, pt, st):
    for (a, b, out, first) in ((k, v, pt, L), (g, q, st, 0)):
        high, low = split_product(a[:, lanes(c)], b[:, lanes(c)])
        out[c, 0, :, first : first + 2 * L] = high
        out[c, 1, :, first : first + 2 * L] = low


def prepare_halo(c, halo, out, first, here):
    high, low = split_product(halo[0, :, lanes(c)], halo[1, :, lanes(c)])
    keep = jnp.where(here, 1.0, 0.0).astype(BF16)
    out[c, 0, :, first : first + L] = high * keep
    out[c, 1, :, first : first + L] = low * keep


def lag_inner(c, pt, st, diag):
    row = lax.broadcasted_iota(jnp.int32, (L, L), 0)
    lane = lax.broadcasted_iota(jnp.int32, (L, L), 1)
    upper = lane >= row
    none = jnp.zeros((CH, L), BF16)
    for r in range(GROUPS):
        rows = slice(CH * r, CH * r + CH)
        p = [[pt[c, part, rows, L * b : L * b + L] for b in (1, 2)] for part in (0, 1)]
        s = [[st[c, part, rows, L * b : L * b + L] for b in (0, 1)] for part in (0, 1)]
        left = jnp.concatenate([p[0][0], p[0][1], p[1][0], p[1][1], p[0][0], p[0][1]], axis=0)
        right = jnp.concatenate(
            [
                jnp.concatenate([s[part][0], s[part][1]], axis=1) if b == 0 else jnp.concatenate([s[part][1], none], axis=1)
                for part in (0, 0, 1)
                for b in (0, 1)
            ],
            axis=0,
        )
        both = dot(left, right, ((0,), (0,)))
        diag[c, r] = jnp.where(upper, both[:, :L], both[:, L:])


def lag_cross(c, pt, st, pb, sb, diag, folded, lag):
    row = lax.broadcasted_iota(jnp.int32, (L, L), 0)
    lane = lax.broadcasted_iota(jnp.int32, (L, L), 1)
    upper = lane >= row
    none = jnp.zeros((CH, L), BF16)
    for r in range(0, GROUPS, 2):
        left, right = [], []
        for e in range(2):
            rows = slice(CH * (r + e), CH * (r + e) + CH)
            p = [pt[c, part, rows, pl.ds(pl.multiple_of(pb * L, L), L)] for part in (0, 1)]
            s = [st[c, part, rows, pl.ds(pl.multiple_of(sb * L, L), L)] for part in (0, 1)]
            for i, j in ((0, 0), (1, 0), (0, 1)):
                left.append(p[i])
                right.append(jnp.concatenate([s[j], none] if e == 0 else [none, s[j]], axis=1))
        both = dot(jnp.concatenate(left, axis=0), jnp.concatenate(right, axis=0), ((0,), (0,)))
        for e in range(2):
            whole = diag[c, r + e] + jnp.where(upper, 0.0, both[:, L * e : L * e + L])
            total = whole[:8]
            for a in range(8, L, 8):
                total = total + pltpu.roll(whole[a : a + 8], L - a, 1)
            folded[8 * (r + e) : 8 * (r + e) + 8, :] = total
    total = folded[pl.ds(0, GROUPS, stride=8), :]
    for a in range(1, 8):
        total = total + pltpu.roll(folded[pl.ds(a, GROUPS, stride=8), :], L - a, 1)
    lag[c] = total


def toeplitz(c, taps, band):
    row = lax.broadcasted_iota(jnp.int32, (L, L), 0)
    lane = lax.broadcasted_iota(jnp.int32, (L, L), 1)
    upper = jnp.where(lane >= row, 1.0, 0.0).astype(BF16)
    for r in range(GROUPS):
        line = taps[c, r : r + 1, :]
        whole = pltpu.roll(jnp.broadcast_to(line, (L, L)), 0, 1, stride=1, stride_axis=0)
        high = whole.astype(BF16)
        low = (whole - high.astype(F32)).astype(BF16)
        for i, part in ((0, high), (1, low)):
            now = part * upper
            band[c, r, L:, L * i : L * i + L] = now
            band[c, r, :L, L * i : L * i + L] = part - now


def convolve(c, pt, st, band, mixed, back):
    for r in range(GROUPS):
        rows = slice(CH * r, CH * r + CH)
        w = band[c, r]
        w_back = jnp.concatenate(
            [
                jnp.concatenate([w[L:, :L], w[:L, :L]], axis=1),
                jnp.concatenate([w[L:, L:], w[:L, L:]], axis=1),
            ],
            axis=0,
        )
        for x, weights, dims, out in ((pt, w, ((1,), (0,)), mixed), (st, w_back, ((1,), (1,)), back)):
            left = jnp.concatenate(
                [x[c, part, rows, L * b : L * b + 2 * L] for part in (0, 1) for b in (0, 1)], axis=0
            )
            got = dot(left, weights, dims)
            for b in (0, 1):
                out[rows, L * b : L * b + L] = (
                    got[CH * b : CH * b + CH, :L]
                    + got[CH * b : CH * b + CH, L:]
                    + got[CH * (2 + b) : CH * (2 + b) + CH, :L]
                )


def finish(c, k, v, g, mixed, back, gq, gk, gv):
    forward = jnp.transpose(mixed[...])
    backward = jnp.transpose(back[...])
    gq[:, lanes(c)] = (g[:, lanes(c)].astype(F32) * forward).astype(BF16)
    gk[:, lanes(c)] = (backward * v[:, lanes(c)].astype(F32)).astype(BF16)
    gv[:, lanes(c)] = (backward * k[:, lanes(c)].astype(F32)).astype(BF16)


def kernel(
    ny, nx, rows_here,
    k_hbm, v_hbm, q_hbm, g_hbm, taps_in, decay_in,
    gq, gk, gv, gf,
    k, v, q, g, kv_halo, qg_halo, pt, st, band, diag, folded, taps, lag, mixed, back,
    mine, gather_x, column, gather_y, partial, reduce_y, final, reduce_x, summed,
    in_sem, kv_send, kv_recv, qg_send, qg_recv, send, recv,
):
    n = ny * nx
    me = lax.axis_index("ctx")
    y, xc = me // nx, me % nx
    core = me % 2
    nxt, prv = (me + 1) % n, (me + n - 1) % n
    tokens = 2 * L
    half = CHUNKS * LANES // 2
    block = nx * rows_here
    groups = taps_in.shape[1]

    at_x = [y * nx + (xc + d) % nx for d in range(1, nx)]
    at_y = [((y + d) % ny) * nx + xc for d in range(1, ny)]

    loads = [
        pltpu.make_async_copy(src, dst, in_sem.at[i])
        for i, (src, dst) in enumerate(((k_hbm, k), (v_hbm, v), (g_hbm, g), (q_hbm, q)))
    ]

    def halo_copies(h, sources, first, dst, sends, recvs, there):
        columns = pl.ds(pl.multiple_of(h * half, LANES), half)
        return [
            pltpu.make_async_remote_copy(
                src_ref=src.at[first : first + L, columns], dst_ref=dst.at[i, :, columns],
                send_sem=sends.at[h, i], recv_sem=recvs.at[h, i],
                device_id={"ctx": there}, device_id_type=MESH,
            )
            for i, src in enumerate(sources)
        ]

    def kv_copies(h):
        return halo_copies(h, (k_hbm, v_hbm), tokens - L, kv_halo, kv_send, kv_recv, nxt)

    def qg_copies(h):
        return halo_copies(h, (g_hbm, q_hbm), 0, qg_halo, qg_send, qg_recv, prv)

    def exchange(which, sources, dst, slot, there):
        for src, device in zip(sources, there):
            pltpu.make_async_remote_copy(
                src_ref=src, dst_ref=dst.at[slot], send_sem=send.at[which], recv_sem=recv.at[which],
                device_id={"ctx": device}, device_id_type=MESH,
            ).start()

    def all_of(which, dst, count):
        return pltpu.make_async_remote_copy(
            src_ref=dst.at[:count], dst_ref=dst.at[:count], send_sem=send.at[which], recv_sem=recv.at[which],
            device_id={"ctx": nxt}, device_id_type=MESH,
        )

    def add_up(slots):
        total = slots[0]
        for i in range(1, slots.shape[0]):
            total = total + slots[i]
        return total

    for copy in loads:
        copy.start()

    barrier = pltpu.get_barrier_semaphore()
    for there in [nxt, prv] + at_x + at_y:
        pl.semaphore_signal(barrier, inc=1, device_id={"ctx": there}, device_id_type=MESH)

    row = lax.broadcasted_iota(jnp.int32, (block, L), 0)
    whole = jnp.zeros((block, L), F32)
    for i in range(rows_here):
        line = jnp.concatenate([taps_in[i : i + 1, :], jnp.zeros((1, L - groups), F32)], axis=1)
        whole = jnp.where(row == xc * rows_here + i, line, whole)
    mine[...] = whole
    gather_x[pl.ds(xc, 1)] = whole[None]

    pl.semaphore_wait(barrier, 2 + (nx - 1) + (ny - 1))
    exchange(0, [mine] * (nx - 1), gather_x, xc, at_x)
    for h in range(2):
        for copy in kv_copies(h) + qg_copies(1 - h):
            copy.start()

    for copy in loads:
        copy.wait()

    def prepare_step(c, carry):
        prepare(c, k, v, g, q, pt, st)
        return carry

    lax.fori_loop(0, CHUNKS, prepare_step, 0)

    def inner_step(c, carry):
        lag_inner(c, pt, st, diag)
        return carry

    lax.fori_loop(0, CHUNKS, inner_step, 0)

    all_of(0, gather_x, nx - 1).wait_recv()
    total = add_up(gather_x)
    column[...] = total
    gather_y[pl.ds(y, 1)] = total[None]
    exchange(1, [column] * (ny - 1), gather_y, y, at_y)

    def kv_arrived(h):
        for copy in kv_copies(h):
            copy.wait_recv()

        def step(i, carry):
            prepare_halo(2 * h + i, kv_halo, pt, 0, me > 0)
            return carry

        lax.fori_loop(0, 2, step, 0)

    def qg_arrived(h):
        for copy in qg_copies(h):
            copy.wait_recv()

        def step(i, carry):
            prepare_halo(2 * h + i, qg_halo, st, 2 * L, me < n - 1)
            return carry

        lax.fori_loop(0, 2, step, 0)

    def cross_step(i, carry):
        h = (i + 1 - core) % 2

        @pl.when(h == 0)
        def _():
            kv_arrived(0)

        @pl.when(h == 1)
        def _():
            qg_arrived(1)

        def step(j, carry):
            lag_cross(2 * h + j, pt, st, 2 * h, 2 * h, diag, folded, lag)
            return carry

        lax.fori_loop(0, 2, step, 0)
        return carry

    lax.fori_loop(0, 2, cross_step, 0)

    per_lag = jnp.transpose(
        jnp.concatenate([lag[c] for c in range(CHUNKS)] + [jnp.zeros((L - CHUNKS * GROUPS, L), F32)], axis=0)
    )
    partial[...] = per_lag.reshape(ny, block, L)
    reduce_y[pl.ds(y, 1)] = partial[pl.ds(y, 1)]
    exchange(2, [partial.at[(y + d) % ny] for d in range(1, ny)], reduce_y, y, at_y)

    all_of(1, gather_y, ny - 1).wait_recv()
    decay = jnp.concatenate([decay_in[...], jnp.zeros((1, L - groups), F32)], axis=1)
    step = lax.broadcasted_iota(jnp.int32, (L, L), 0).astype(F32)
    turned = jnp.transpose(gather_y[...].reshape(L, L) * jnp.exp(-decay * step))
    for c in range(CHUNKS):
        taps[c] = turned[GROUPS * c : GROUPS * c + GROUPS]

    def output_step(c, carry):
        toeplitz(c, taps, band)
        convolve(c, pt, st, band, mixed, back)
        finish(c, k, v, g, mixed, back, gq, gk, gv)
        return carry

    def output_half(i):
        h = (i + core) % 2

        @pl.when(h == 0)
        def _():
            qg_arrived(0)

        @pl.when(h == 1)
        def _():
            kv_arrived(1)

        lax.fori_loop(2 * h, 2 * h + 2, output_step, 0)

    output_half(0)
    all_of(2, reduce_y, ny - 1).wait_recv()
    total = add_up(reduce_y)
    final[...] = total
    reduce_x[pl.ds(xc, 1)] = total[None]
    exchange(3, [final] * (nx - 1), reduce_x, xc, at_x)
    output_half(1)

    all_of(3, reduce_x, nx - 1).wait_recv()
    summed[...] = add_up(reduce_x)
    lag_index = (me * rows_here + lax.broadcasted_iota(jnp.int32, (rows_here, L), 0)).astype(F32)
    share = summed[pl.ds(xc * rows_here, rows_here), :] * jnp.exp(-decay * lag_index) / float(tokens * n)
    gf[...] = share[:, :groups]

    for h in range(2):
        for copy in kv_copies(h) + qg_copies(h):
            copy.wait_send()
    all_of(0, gather_x, nx - 1).wait_send()
    all_of(1, gather_y, ny - 1).wait_send()
    all_of(2, reduce_y, ny - 1).wait_send()
    all_of(3, reduce_x, nx - 1).wait_send()


def write_out(*refs):
    count = len(refs) // 2
    sems = refs[-1]
    copies = [pltpu.make_async_copy(refs[i], refs[count + i], sems.at[i]) for i in range(count)]
    for copy in copies:
        copy.start()
    for copy in copies:
        copy.wait()


def on_device(ny, nx, query_act, key_act, value_act, grad_gated, filter_taps, decay_rate):
    tokens, channels = query_act.shape
    rows_here, groups = filter_taps.shape
    block = nx * rows_here
    whole = jax.ShapeDtypeStruct((tokens, channels), BF16)
    shapes = (whole, whole, whole, jax.ShapeDtypeStruct((rows_here, groups), F32))
    vmem = pl.BlockSpec(memory_space=pltpu.VMEM)
    hbm = pl.BlockSpec(memory_space=pl.ANY)
    dma = pltpu.SemaphoreType.DMA
    inner = pltpu.VMEM((tokens, channels), BF16)
    halo = pltpu.VMEM((2, L, channels), BF16)
    wide = pltpu.VMEM((CHUNKS, 2, LANES, 3 * L), BF16)
    rows = pltpu.VMEM((block, L), F32)
    by_x, by_y = pltpu.VMEM((nx, block, L), F32), pltpu.VMEM((ny, block, L), F32)
    results = pl.pallas_call(
        functools.partial(kernel, ny, nx, rows_here),
        out_shape=shapes,
        in_specs=[hbm] * 4 + [vmem] * 2,
        out_specs=(vmem,) * 4,
        scratch_shapes=[
            inner, inner, inner, inner, halo, halo, wide, wide,
            pltpu.VMEM((CHUNKS, GROUPS, 2 * L, 2 * L), BF16),
            pltpu.VMEM((CHUNKS, GROUPS, L, L), F32),
            pltpu.VMEM((8 * GROUPS, L), F32),
            pltpu.VMEM((CHUNKS, GROUPS, L), F32),
            pltpu.VMEM((CHUNKS, GROUPS, L), F32),
            pltpu.VMEM((LANES, tokens), F32),
            pltpu.VMEM((LANES, tokens), F32),
            rows, by_x, rows, by_y, by_y, by_y, rows, by_x, rows,
            dma((4,)), dma((2, 2)), dma((2, 2)), dma((2, 2)), dma((2, 2)), dma((4,)), dma((4,)),
        ],
        compiler_params=pltpu.CompilerParams(
            collective_id=0, has_side_effects=True, vmem_limit_bytes=VMEM_LIMIT
        ),
    )(key_act, value_act, query_act, grad_gated, filter_taps, decay_rate.reshape(1, groups))
    return pl.pallas_call(
        write_out,
        out_shape=shapes,
        in_specs=[vmem] * 4,
        out_specs=(hbm,) * 4,
        scratch_shapes=[dma((4,))],
        compiler_params=pltpu.CompilerParams(vmem_limit_bytes=4 * 1024 * 1024),
    )(*results)


def solution(mesh):
    n = mesh.shape["ctx"]
    nx = 8 if n >= 64 else 4
    return jax.shard_map(
        functools.partial(on_device, n // nx, nx),
        mesh=mesh,
        in_specs=(P("ctx", "tp"),) * 5 + (P("tp"),),
        out_specs=(P("ctx", "tp"),) * 4,
        check_vma=False,
    )
```

```python
import functools

import jax
import jax.numpy as jnp
from jax import lax
from jax.experimental import pallas as pl
from jax.experimental.pallas import tpu as pltpu
from jax.sharding import PartitionSpec as P

L = 128
CH = 16
LANES = 128
CHUNKS = 4
GROUPS = LANES // CH
VMEM_LIMIT = 53 * 1024 * 1024
MESH = pl.DeviceIdType.MESH
F32, BF16 = jnp.float32, jnp.bfloat16


def dot(a, b, dims):
    return lax.dot_general(a, b, (dims, ((), ())), preferred_element_type=F32)


def flip(x):
    turn = 7 - lax.broadcasted_iota(jnp.int32, (8, LANES), 0)
    tiles = [jnp.take_along_axis(x[i : i + 8], turn, axis=0) for i in range(0, x.shape[0], 8)]
    return jnp.concatenate(tiles[::-1], axis=0)


def split_product(a, b, backward):
    whole = a.astype(F32) * b.astype(F32)
    whole = jnp.transpose(flip(whole) if backward else whole)
    high = whole.astype(BF16)
    return high, (whole - high.astype(F32)).astype(BF16)


def lanes(c):
    return pl.ds(pl.multiple_of(c * LANES, LANES), LANES)


def prepare(c, k, v, g, q, pt, st):
    for (a, b, out, backward) in ((k, v, pt, False), (g, q, st, True)):
        high, low = split_product(a[:, lanes(c)], b[:, lanes(c)], backward)
        out[c, 0, :, L:] = high
        out[c, 1, :, L:] = low


def prepare_halo(c, halo, out, backward, here):
    high, low = split_product(halo[0, :, lanes(c)], halo[1, :, lanes(c)], backward)
    keep = jnp.where(here, 1.0, 0.0).astype(BF16)
    out[c, 0, :, :L] = high * keep
    out[c, 1, :, :L] = low * keep


def lag_inner(c, pt, st, diag):
    row = lax.broadcasted_iota(jnp.int32, (L, L), 0)
    lane = lax.broadcasted_iota(jnp.int32, (L, L), 1)
    upper = lane + row < L
    none = jnp.zeros((CH, L), BF16)
    for r in range(GROUPS):
        rows = slice(CH * r, CH * r + CH)
        p = [[pt[c, part, rows, L * b : L * b + L] for b in (1, 2)] for part in (0, 1)]
        s = [[st[c, part, rows, L * b : L * b + L] for b in (2, 1)] for part in (0, 1)]
        left = jnp.concatenate([p[0][0], p[0][1], p[1][0], p[1][1], p[0][0], p[0][1]], axis=0)
        right = jnp.concatenate(
            [
                jnp.concatenate([s[part][0], s[part][1]], axis=1) if b == 0 else jnp.concatenate([s[part][1], none], axis=1)
                for part in (0, 0, 1)
                for b in (0, 1)
            ],
            axis=0,
        )
        both = dot(left, right, ((0,), (0,)))
        diag[c, r] = jnp.where(upper, both[:, :L], both[:, L:])


def lag_cross(c, pt, st, pb, sb, diag, folded, lag):
    row = lax.broadcasted_iota(jnp.int32, (L, L), 0)
    lane = lax.broadcasted_iota(jnp.int32, (L, L), 1)
    upper = lane + row < L
    none = jnp.zeros((CH, L), BF16)
    for r in range(0, GROUPS, 2):
        left, right = [], []
        for e in range(2):
            rows = slice(CH * (r + e), CH * (r + e) + CH)
            p = [pt[c, part, rows, pl.ds(pl.multiple_of(pb * L, L), L)] for part in (0, 1)]
            s = [st[c, part, rows, pl.ds(pl.multiple_of(sb * L, L), L)] for part in (0, 1)]
            for i, j in ((0, 0), (1, 0), (0, 1)):
                left.append(p[i])
                right.append(jnp.concatenate([s[j], none] if e == 0 else [none, s[j]], axis=1))
        both = dot(jnp.concatenate(left, axis=0), jnp.concatenate(right, axis=0), ((0,), (0,)))
        for e in range(2):
            whole = diag[c, r + e] + jnp.where(upper, 0.0, both[:, L * e : L * e + L])
            total = whole[:8]
            for a in range(8, L, 8):
                total = total + pltpu.roll(whole[a : a + 8], a, 1)
            folded[8 * (r + e) : 8 * (r + e) + 8, :] = total
    total = folded[pl.ds(0, GROUPS, stride=8), :]
    for a in range(1, 8):
        total = total + pltpu.roll(folded[pl.ds(a, GROUPS, stride=8), :], a, 1)
    lag[c] = total


def toeplitz(c, taps, band):
    row = lax.broadcasted_iota(jnp.int32, (L, L), 0)
    lane = lax.broadcasted_iota(jnp.int32, (L, L), 1)
    upper = jnp.where(lane >= row, 1.0, 0.0).astype(BF16)
    for r in range(GROUPS):
        line = taps[c, r : r + 1, :]
        whole = pltpu.roll(jnp.broadcast_to(line, (L, L)), 0, 1, stride=1, stride_axis=0)
        high = whole.astype(BF16)
        low = (whole - high.astype(F32)).astype(BF16)
        for i, part in ((0, high), (1, low)):
            now = part * upper
            band[c, r, L:, L * i : L * i + L] = now
            band[c, r, :L, L * i : L * i + L] = part - now


def convolve(c, pt, st, band, mixed, back):
    for r in range(GROUPS):
        rows = slice(CH * r, CH * r + CH)
        left = [x[c, part, rows, L * b : L * b + 2 * L] for x in (pt, st) for part in (0, 1) for b in (0, 1)]
        got = dot(jnp.concatenate(left, axis=0), band[c, r], ((1,), (0,)))
        for i, out in enumerate((mixed, back)):
            for b in (0, 1):
                high, low = CH * (4 * i + b), CH * (4 * i + 2 + b)
                out[rows, L * b : L * b + L] = (
                    got[high : high + CH, :L] + got[high : high + CH, L:] + got[low : low + CH, :L]
                )


def finish(c, k, v, g, mixed, back, gq, gk, gv):
    forward = jnp.transpose(mixed[...])
    backward = flip(jnp.transpose(back[...]))
    gq[:, lanes(c)] = (g[:, lanes(c)].astype(F32) * forward).astype(BF16)
    gk[:, lanes(c)] = (backward * v[:, lanes(c)].astype(F32)).astype(BF16)
    gv[:, lanes(c)] = (backward * k[:, lanes(c)].astype(F32)).astype(BF16)


def kernel(
    ny, nx, rows_here,
    k_hbm, v_hbm, q_hbm, g_hbm, taps_in, decay_in,
    gq, gk, gv, gf,
    k, v, q, g, kv_halo, qg_halo, pt, st, band, diag, folded, taps, lag, mixed, back,
    gather, partial, reduced, all_taps,
    in_sem, kv_send, kv_recv, qg_send, qg_recv, send, recv, ready,
):
    n = ny * nx * 2
    me = lax.axis_index("ctx")
    chip, core = me // 2, me % 2
    nxt, prv = (me + 1) % n, (me + n - 1) % n
    tokens = 2 * L
    half = CHUNKS * LANES // 2
    groups = taps_in.shape[1]

    def hops(dy, dx):
        return min(dy, ny - dy) + min(dx, nx - dx)

    steps = [(dy, dx) for dy in range(ny) for dx in range(nx) if dy or dx]
    steps.sort(key=lambda step: -hops(*step))
    chips = [((chip // nx + dy) % ny) * nx + (chip % nx + dx) % nx for dy, dx in steps]
    everyone = [device for there in chips for device in (2 * there, 2 * there + 1)] + [me + 1 - 2 * core]

    loads = [
        pltpu.make_async_copy(src, dst, in_sem.at[i])
        for i, (src, dst) in enumerate(((k_hbm, k), (v_hbm, v), (g_hbm, g), (q_hbm, q)))
    ]

    def halo_copies(piece, lead, sources, first, dst, sends, recvs, there):
        columns = slice(lead + piece * LANES, lead + (piece + 1) * LANES) if piece < 2 else slice(half - lead, 2 * half - lead)
        return [
            pltpu.make_async_remote_copy(
                src_ref=src.at[first : first + L, columns], dst_ref=dst.at[i, :, columns],
                send_sem=sends.at[piece, i], recv_sem=recvs.at[piece, i],
                device_id={"ctx": there}, device_id_type=MESH,
            )
            for i, src in enumerate(sources)
        ]

    def kv_copies(piece):
        return halo_copies(piece, 0, (k, v), tokens - L, kv_halo, kv_send, kv_recv, nxt)

    def qg_copies(piece):
        return halo_copies(piece, half, (g, q), 0, qg_halo, qg_send, qg_recv, prv)

    def send_to(which, src, dst, there):
        return pltpu.make_async_remote_copy(
            src_ref=src, dst_ref=dst, send_sem=send.at[which], recv_sem=recv.at[which],
            device_id={"ctx": there}, device_id_type=MESH,
        )

    def bytes_of(which, slots):
        return send_to(which, slots, slots, nxt)

    for copy in loads:
        copy.start()

    def along_y(dy):
        return 2 * (((chip // nx + ny + dy) % ny) * nx + chip % nx) + core

    row = [2 * ((chip // nx) * nx + (chip % nx + dx) % nx) for dx in range(nx)]
    def around(*distances):
        return sorted({d % ny for r in distances for d in (r, -r)} - {0})

    near = [nxt, prv, me + 1 - 2 * core] + [along_y(d) for d in around(1, 2)]
    row_mates = [me + 1 - 2 * core] + [there + c for there in row[1:] for c in (0, 1)]
    near += row_mates[1:]
    barrier = pltpu.get_barrier_semaphore()
    for there in near:
        pl.semaphore_signal(barrier, inc=1, device_id={"ctx": there}, device_id_type=MESH)

    mine = jnp.concatenate([taps_in[...], jnp.zeros((rows_here, L - groups), F32)], axis=1)
    place = me % (2 * nx)
    gather[pl.ds(chip // nx, 1), pl.ds(place, 1)] = mine[None, None]

    for copy in loads:
        copy.wait()
    pl.semaphore_wait(barrier, len(near))
    def tell(which, *distances):
        for d in around(*distances):
            pl.semaphore_signal(ready.at[which], inc=1, device_id={"ctx": along_y(d)}, device_id_type=MESH)

    my_row = gather.at[chip // nx]
    for there in row_mates:
        send_to(0, my_row.at[place], my_row.at[place], there).start()
    for piece in range(3):
        for copy in kv_copies(piece) + qg_copies(piece):
            copy.start()
    tell(0, 1, 2)

    def prepare_step(c, carry):
        prepare(c, k, v, g, q, pt, st)
        return carry

    lax.fori_loop(0, CHUNKS, prepare_step, 0)
    pl.semaphore_wait(ready.at[0], len(around(1, 2)))
    tell(1, 2)

    def inner_step(c, carry):
        lag_inner(c, pt, st, diag)
        return carry

    lax.fori_loop(0, CHUNKS, inner_step, 0)
    bytes_of(0, my_row.at[: 2 * nx - 1]).wait_recv()
    for d in sorted(range(1, ny), key=lambda d: -hops(d, 0)):
        send_to(1, my_row, my_row, along_y(d)).start()

    def kv_arrived(piece, chunks):
        for copy in kv_copies(piece):
            copy.wait_recv()
        for c in chunks:
            prepare_halo(c, kv_halo, pt, False, me > 0)

    def qg_arrived(piece, chunks):
        for copy in qg_copies(piece):
            copy.wait_recv()
        for c in chunks:
            prepare_halo(c, qg_halo, st, True, me < n - 1)

    def cross_step(i, carry):
        c = (i + 2 - 2 * core) % CHUNKS
        h = c // 2
        for piece in range(2):

            @pl.when(c == piece)
            def _():
                kv_arrived(piece, [piece])

            @pl.when(c == 2 + piece)
            def _():
                qg_arrived(piece, [2 + piece])

        lag_cross(c, pt, st, 2 * h, 2 - 2 * h, diag, folded, lag)
        return carry

    lax.fori_loop(0, CHUNKS, cross_step, 0)

    per_lag = jnp.transpose(
        jnp.concatenate([lag[c] for c in range(CHUNKS)] + [jnp.zeros((L - CHUNKS * GROUPS, L), F32)], axis=0)
    )
    for i in range(n):
        partial[i] = per_lag[L - rows_here * (i + 1) : L - rows_here * i]
    reduced[pl.ds(me, 1)] = partial[pl.ds(me, 1)]
    pl.semaphore_wait(ready.at[1], len(around(2)))
    for there in everyone:
        send_to(2, partial.at[there], reduced.at[me], there).start()

    bytes_of(1, gather.at[: ny - 1]).wait_recv()
    for i in range(n):
        all_taps[rows_here * i : rows_here * (i + 1), :] = gather[i // (2 * nx), i % (2 * nx)]
    decay = jnp.concatenate([decay_in[...], jnp.zeros((1, L - groups), F32)], axis=1)
    step = lax.broadcasted_iota(jnp.int32, (L, L), 0).astype(F32)
    turned = jnp.transpose(all_taps[...] * jnp.exp(-decay * step))
    for c in range(CHUNKS):
        taps[c] = turned[GROUPS * c : GROUPS * c + GROUPS]

    def output_step(c, carry):
        toeplitz(c, taps, band)
        convolve(c, pt, st, band, mixed, back)
        finish(c, k, v, g, mixed, back, gq, gk, gv)
        return carry

    def output_half(i):
        h = (i + core) % 2

        @pl.when(h == 0)
        def _():
            qg_arrived(2, [0, 1])

        @pl.when(h == 1)
        def _():
            kv_arrived(2, [2, 3])

        lax.fori_loop(2 * h, 2 * h + 2, output_step, 0)

    output_half(0)
    output_half(1)

    bytes_of(2, reduced.at[: n - 1]).wait_recv()
    total = jnp.sum(reduced[...], axis=0)
    total = jnp.concatenate([total[i : i + 1] for i in reversed(range(rows_here))], axis=0)
    lag_index = (me * rows_here + lax.broadcasted_iota(jnp.int32, (rows_here, L), 0)).astype(F32)
    gf[...] = (total * jnp.exp(-decay * lag_index) / float(tokens * n))[:, :groups]

    for piece in range(3):
        for copy in kv_copies(piece) + qg_copies(piece):
            copy.wait_send()
    bytes_of(0, my_row.at[: 2 * nx - 1]).wait_send()
    bytes_of(1, gather.at[: ny - 1]).wait_send()
    bytes_of(2, reduced.at[: n - 1]).wait_send()


def write_out(*refs):
    count = len(refs) // 2
    sems = refs[-1]
    copies = [pltpu.make_async_copy(refs[i], refs[count + i], sems.at[i]) for i in range(count)]
    for copy in copies:
        copy.start()
    for copy in copies:
        copy.wait()


def on_device(ny, nx, query_act, key_act, value_act, grad_gated, filter_taps, decay_rate):
    tokens, channels = query_act.shape
    rows_here, groups = filter_taps.shape
    whole = jax.ShapeDtypeStruct((tokens, channels), BF16)
    shapes = (whole, whole, whole, jax.ShapeDtypeStruct((rows_here, groups), F32))
    vmem = pl.BlockSpec(memory_space=pltpu.VMEM)
    hbm = pl.BlockSpec(memory_space=pl.ANY)
    dma = pltpu.SemaphoreType.DMA
    inner = pltpu.VMEM((tokens, channels), BF16)
    halo = pltpu.VMEM((2, L, channels), BF16)
    wide = pltpu.VMEM((CHUNKS, 2, LANES, 3 * L), BF16)
    by_device = pltpu.VMEM((2 * ny * nx, rows_here, L), F32)
    results = pl.pallas_call(
        functools.partial(kernel, ny, nx, rows_here),
        out_shape=shapes,
        in_specs=[hbm] * 4 + [vmem] * 2,
        out_specs=(vmem,) * 4,
        scratch_shapes=[
            inner, inner, inner, inner, halo, halo, wide, wide,
            pltpu.VMEM((CHUNKS, GROUPS, 2 * L, 2 * L), BF16),
            pltpu.VMEM((CHUNKS, GROUPS, L, L), F32),
            pltpu.VMEM((8 * GROUPS, L), F32),
            pltpu.VMEM((CHUNKS, GROUPS, L), F32),
            pltpu.VMEM((CHUNKS, GROUPS, L), F32),
            pltpu.VMEM((LANES, tokens), F32),
            pltpu.VMEM((LANES, tokens), F32),
            pltpu.VMEM((ny, 2 * nx, rows_here, L), F32),
            by_device, by_device,
            pltpu.VMEM((L, L), F32),
            dma((6,)), dma((3, 2)), dma((3, 2)), dma((3, 2)), dma((3, 2)), dma((3,)), dma((3,)), pltpu.SemaphoreType.REGULAR((2,)),
        ],
        compiler_params=pltpu.CompilerParams(
            collective_id=0, has_side_effects=True, vmem_limit_bytes=VMEM_LIMIT
        ),
    )(key_act, value_act, query_act, grad_gated, filter_taps, decay_rate.reshape(1, groups))
    return pl.pallas_call(
        write_out,
        out_shape=shapes,
        in_specs=[vmem] * 4,
        out_specs=(hbm,) * 4,
        scratch_shapes=[dma((4,))],
        compiler_params=pltpu.CompilerParams(vmem_limit_bytes=4 * 1024 * 1024),
    )(*results)


def solution(mesh):
    chips = mesh.shape["ctx"] // 2
    nx = 4 if chips >= 32 else 2
    return jax.shard_map(
        functools.partial(on_device, chips // nx, nx),
        mesh=mesh,
        in_specs=(P("ctx", "tp"),) * 5 + (P("tp"),),
        out_specs=(P("ctx", "tp"),) * 4,
        check_vma=False,
    )
```

```python
import functools

import jax
import jax.numpy as jnp
from jax import lax
from jax.experimental import pallas as pl
from jax.experimental.pallas import tpu as pltpu
from jax.sharding import PartitionSpec as P

L = 128
CH = 16
LANES = 128
CHUNKS = 4
GROUPS = LANES // CH
VMEM_LIMIT = 32 * 1024 * 1024
MESH = pl.DeviceIdType.MESH
F32, BF16 = jnp.float32, jnp.bfloat16


def dot(a, b, dims):
    return lax.dot_general(a, b, (dims, ((), ())), preferred_element_type=F32)


def flip(x):
    turn = 7 - lax.broadcasted_iota(jnp.int32, (8, LANES), 0)
    tiles = [jnp.take_along_axis(x[i : i + 8], turn, axis=0) for i in range(0, x.shape[0], 8)]
    return jnp.concatenate(tiles[::-1], axis=0)


def split_product(a, b, backward):
    whole = a.astype(F32) * b.astype(F32)
    whole = jnp.transpose(flip(whole) if backward else whole)
    high = whole.astype(BF16)
    return high, (whole - high.astype(F32)).astype(BF16)


def lanes(c):
    return pl.ds(pl.multiple_of(c * LANES, LANES), LANES)


def prepare(c, k, v, g, q, pt, st):
    for (a, b, out, backward) in ((k, v, pt, False), (g, q, st, True)):
        high, low = split_product(a[:, lanes(c)], b[:, lanes(c)], backward)
        out[c, 0, :, L:] = high
        out[c, 1, :, L:] = low


def prepare_halo(c, halo, out, backward, here):
    high, low = split_product(halo[0, :, lanes(c)], halo[1, :, lanes(c)], backward)
    keep = jnp.where(here, 1.0, 0.0).astype(BF16)
    out[c, 0, :, :L] = high * keep
    out[c, 1, :, :L] = low * keep


def lag_inner(c, pt, st, diag):
    row = lax.broadcasted_iota(jnp.int32, (L, L), 0)
    lane = lax.broadcasted_iota(jnp.int32, (L, L), 1)
    upper = lane + row < L
    none = jnp.zeros((CH, L), BF16)
    for r in range(GROUPS):
        rows = slice(CH * r, CH * r + CH)
        p = [[pt[c, part, rows, L * b : L * b + L] for b in (1, 2)] for part in (0, 1)]
        s = [[st[c, part, rows, L * b : L * b + L] for b in (2, 1)] for part in (0, 1)]
        left = jnp.concatenate([p[0][0], p[0][1], p[1][0], p[1][1], p[0][0], p[0][1]], axis=0)
        right = jnp.concatenate(
            [
                jnp.concatenate([s[part][0], s[part][1]], axis=1) if b == 0 else jnp.concatenate([s[part][1], none], axis=1)
                for part in (0, 0, 1)
                for b in (0, 1)
            ],
            axis=0,
        )
        both = dot(left, right, ((0,), (0,)))
        diag[c, r] = jnp.where(upper, both[:, :L], both[:, L:])


def lag_cross(c, pt, st, pb, sb, diag, folded, lag):
    row = lax.broadcasted_iota(jnp.int32, (L, L), 0)
    lane = lax.broadcasted_iota(jnp.int32, (L, L), 1)
    upper = lane + row < L
    none = jnp.zeros((CH, L), BF16)
    for r in range(0, GROUPS, 2):
        left, right = [], []
        for e in range(2):
            rows = slice(CH * (r + e), CH * (r + e) + CH)
            p = [pt[c, part, rows, pl.ds(pl.multiple_of(pb * L, L), L)] for part in (0, 1)]
            s = [st[c, part, rows, pl.ds(pl.multiple_of(sb * L, L), L)] for part in (0, 1)]
            for i, j in ((0, 0), (1, 0), (0, 1)):
                left.append(p[i])
                right.append(jnp.concatenate([s[j], none] if e == 0 else [none, s[j]], axis=1))
        both = dot(jnp.concatenate(left, axis=0), jnp.concatenate(right, axis=0), ((0,), (0,)))
        for e in range(2):
            whole = diag[c, r + e] + jnp.where(upper, 0.0, both[:, L * e : L * e + L])
            total = whole[:8]
            for a in range(8, L, 8):
                total = total + pltpu.roll(whole[a : a + 8], a, 1)
            folded[8 * (r + e) : 8 * (r + e) + 8, :] = total
    total = folded[pl.ds(0, GROUPS, stride=8), :]
    for a in range(1, 8):
        total = total + pltpu.roll(folded[pl.ds(a, GROUPS, stride=8), :], a, 1)
    lag[c] = total


def toeplitz(c, taps, band):
    row = lax.broadcasted_iota(jnp.int32, (L, L), 0)
    lane = lax.broadcasted_iota(jnp.int32, (L, L), 1)
    upper = jnp.where(lane >= row, 1.0, 0.0).astype(BF16)
    for r in range(GROUPS):
        line = taps[c, r : r + 1, :]
        whole = pltpu.roll(jnp.broadcast_to(line, (L, L)), 0, 1, stride=1, stride_axis=0)
        high = whole.astype(BF16)
        low = (whole - high.astype(F32)).astype(BF16)
        for i, part in ((0, high), (1, low)):
            now = part * upper
            band[c, r, L:, L * i : L * i + L] = now
            band[c, r, :L, L * i : L * i + L] = part - now


def convolve(c, pt, st, band, mixed, back):
    for r in range(GROUPS):
        rows = slice(CH * r, CH * r + CH)
        left = [x[c, part, rows, L * b : L * b + 2 * L] for x in (pt, st) for part in (0, 1) for b in (0, 1)]
        got = dot(jnp.concatenate(left, axis=0), band[c, r], ((1,), (0,)))
        for i, out in enumerate((mixed, back)):
            for b in (0, 1):
                high, low = CH * (4 * i + b), CH * (4 * i + 2 + b)
                out[rows, L * b : L * b + L] = (
                    got[high : high + CH, :L] + got[high : high + CH, L:] + got[low : low + CH, :L]
                )


def finish(c, k, v, g, mixed, back, gq, gk, gv):
    forward = jnp.transpose(mixed[...])
    backward = flip(jnp.transpose(back[...]))
    gq[:, lanes(c)] = (g[:, lanes(c)].astype(F32) * forward).astype(BF16)
    gk[:, lanes(c)] = (backward * v[:, lanes(c)].astype(F32)).astype(BF16)
    gv[:, lanes(c)] = (backward * k[:, lanes(c)].astype(F32)).astype(BF16)


def kernel(
    ny, nx, rows_here,
    k_hbm, v_hbm, q_hbm, g_hbm, taps_hbm, decay_hbm,
    gq, gk, gv, gf,
    k, v, q, g, kv_halo, qg_halo, pt, st, band, diag, folded, taps, lag, mixed, back,
    taps_in, decay_in, gather, partial, reduced, all_taps,
    in_sem, kv_send, kv_recv, qg_send, qg_recv, send, recv, ready,
):
    n = ny * nx * 2
    me = lax.axis_index("ctx")
    chip, core = me // 2, me % 2
    nxt, prv = (me + 1) % n, (me + n - 1) % n
    tokens = 2 * L
    half = CHUNKS * LANES // 2
    groups = taps_hbm.shape[1]

    def hops(dy, dx):
        return min(dy, ny - dy) + min(dx, nx - dx)

    steps = [(dy, dx) for dy in range(ny) for dx in range(nx) if dy or dx]
    steps.sort(key=lambda step: -hops(*step))
    chips = [((chip // nx + dy) % ny) * nx + (chip % nx + dx) % nx for dy, dx in steps]
    everyone = [device for there in chips for device in (2 * there, 2 * there + 1)] + [me + 1 - 2 * core]

    loads = [
        pltpu.make_async_copy(src, dst, in_sem.at[i])
        for i, (src, dst) in enumerate(((k_hbm, k), (v_hbm, v), (g_hbm, g), (q_hbm, q)))
    ]

    def halo_copies(piece, lead, sources, first, dst, sends, recvs, there):
        columns = slice(lead + piece * LANES, lead + (piece + 1) * LANES) if piece < 2 else slice(half - lead, 2 * half - lead)
        return [
            pltpu.make_async_remote_copy(
                src_ref=src.at[first : first + L, columns], dst_ref=dst.at[i, :, columns],
                send_sem=sends.at[piece, i], recv_sem=recvs.at[piece, i],
                device_id={"ctx": there}, device_id_type=MESH,
            )
            for i, src in enumerate(sources)
        ]

    def kv_copies(piece):
        return halo_copies(piece, 0, (k, v), tokens - L, kv_halo, kv_send, kv_recv, nxt)

    def qg_copies(piece):
        return halo_copies(piece, half, (g, q), 0, qg_halo, qg_send, qg_recv, prv)

    def send_to(which, src, dst, there):
        return pltpu.make_async_remote_copy(
            src_ref=src, dst_ref=dst, send_sem=send.at[which], recv_sem=recv.at[which],
            device_id={"ctx": there}, device_id_type=MESH,
        )

    def bytes_of(which, slots):
        return send_to(which, slots, slots, nxt)

    small = [
        pltpu.make_async_copy(taps_hbm, taps_in, in_sem.at[4]),
        pltpu.make_async_copy(decay_hbm, decay_in, in_sem.at[5]),
    ]
    for copy in small + loads:
        copy.start()

    def along_y(dy):
        return 2 * (((chip // nx + ny + dy) % ny) * nx + chip % nx) + core

    row = [2 * ((chip // nx) * nx + (chip % nx + dx) % nx) for dx in range(nx)]
    def around(*distances):
        return sorted({d % ny for r in distances for d in (r, -r)} - {0})

    near = [nxt, prv, me + 1 - 2 * core] + [along_y(d) for d in around(1, 2)]
    row_mates = [me + 1 - 2 * core] + [there + c for there in row[1:] for c in (0, 1)]
    near += row_mates[1:]
    barrier = pltpu.get_barrier_semaphore()
    for there in near:
        pl.semaphore_signal(barrier, inc=1, device_id={"ctx": there}, device_id_type=MESH)

    for copy in small:
        copy.wait()
    mine = jnp.concatenate([taps_in[...], jnp.zeros((rows_here, L - groups), F32)], axis=1)
    place = me % (2 * nx)
    gather[pl.ds(chip // nx, 1), pl.ds(place, 1)] = mine[None, None]

    for copy in loads:
        copy.wait()
    def prepare_step(c, carry):
        prepare(c, k, v, g, q, pt, st)
        return carry

    lax.fori_loop(0, CHUNKS, prepare_step, 0)

    pl.semaphore_wait(barrier, len(near))
    def tell(which, *distances):
        for d in around(*distances):
            pl.semaphore_signal(ready.at[which], inc=1, device_id={"ctx": along_y(d)}, device_id_type=MESH)

    my_row = gather.at[chip // nx]
    for there in row_mates:
        send_to(0, my_row.at[place], my_row.at[place], there).start()
    for piece in range(2):
        for copy in kv_copies(piece) + qg_copies(piece):
            copy.start()
    tell(0, 1, 2)
    for copy in kv_copies(2) + qg_copies(2):
        copy.start()

    def inner_step(c, carry):
        lag_inner(c, pt, st, diag)
        return carry

    lax.fori_loop(0, CHUNKS, inner_step, 0)
    pl.semaphore_wait(ready.at[0], len(around(1, 2)))
    tell(1, 2)

    def kv_arrived(piece, chunks):
        for copy in kv_copies(piece):
            copy.wait_recv()
        for c in chunks:
            prepare_halo(c, kv_halo, pt, False, me > 0)

    def qg_arrived(piece, chunks):
        for copy in qg_copies(piece):
            copy.wait_recv()
        for c in chunks:
            prepare_halo(c, qg_halo, st, True, me < n - 1)

    def cross_step(i, carry):
        c = (i + 2 - 2 * core) % CHUNKS
        h = c // 2
        for piece in range(2):

            @pl.when(c == piece)
            def _():
                kv_arrived(piece, [piece])

            @pl.when(c == 2 + piece)
            def _():
                qg_arrived(piece, [2 + piece])

        lag_cross(c, pt, st, 2 * h, 2 - 2 * h, diag, folded, lag)
        return carry

    lax.fori_loop(0, 2, cross_step, 0)

    bytes_of(0, my_row.at[: 2 * nx - 1]).wait_recv()
    for d in sorted(range(1, ny), key=lambda d: -hops(d, 0)):
        send_to(1, my_row, my_row, along_y(d)).start()

    lax.fori_loop(2, CHUNKS, cross_step, 0)

    per_lag = jnp.transpose(
        jnp.concatenate([lag[c] for c in range(CHUNKS)] + [jnp.zeros((L - CHUNKS * GROUPS, L), F32)], axis=0)
    )
    for i in range(n):
        partial[i] = per_lag[L - rows_here * (i + 1) : L - rows_here * i]
    reduced[pl.ds(me, 1)] = partial[pl.ds(me, 1)]
    pl.semaphore_wait(ready.at[1], len(around(2)))
    for there in everyone:
        send_to(2, partial.at[there], reduced.at[me], there).start()

    bytes_of(1, gather.at[: ny - 1]).wait_recv()
    for i in range(n):
        all_taps[rows_here * i : rows_here * (i + 1), :] = gather[i // (2 * nx), i % (2 * nx)]
    decay = jnp.concatenate([decay_in[...], jnp.zeros((1, L - groups), F32)], axis=1)
    step = lax.broadcasted_iota(jnp.int32, (L, L), 0).astype(F32)
    turned = jnp.transpose(all_taps[...] * jnp.exp(-decay * step))
    for c in range(CHUNKS):
        taps[c] = turned[GROUPS * c : GROUPS * c + GROUPS]

    def output_step(c, carry):
        toeplitz(c, taps, band)
        convolve(c, pt, st, band, mixed, back)
        finish(c, k, v, g, mixed, back, gq, gk, gv)
        return carry

    def output_half(i):
        h = (i + core) % 2

        @pl.when(h == 0)
        def _():
            qg_arrived(2, [0, 1])

        @pl.when(h == 1)
        def _():
            kv_arrived(2, [2, 3])

        lax.fori_loop(2 * h, 2 * h + 2, output_step, 0)

    output_half(0)
    output_half(1)

    bytes_of(2, reduced.at[: n - 1]).wait_recv()
    total = jnp.sum(reduced[...], axis=0)
    total = jnp.concatenate([total[i : i + 1] for i in reversed(range(rows_here))], axis=0)
    lag_index = (me * rows_here + lax.broadcasted_iota(jnp.int32, (rows_here, L), 0)).astype(F32)
    gf[...] = (total * jnp.exp(-decay * lag_index) / float(tokens * n))[:, :groups]

    for piece in range(3):
        for copy in kv_copies(piece) + qg_copies(piece):
            copy.wait_send()
    bytes_of(0, my_row.at[: 2 * nx - 1]).wait_send()
    bytes_of(1, gather.at[: ny - 1]).wait_send()
    bytes_of(2, reduced.at[: n - 1]).wait_send()


def write_out(*refs):
    count = len(refs) // 2
    sems = refs[-1]
    copies = [pltpu.make_async_copy(refs[i], refs[count + i], sems.at[i]) for i in range(count)]
    for copy in copies:
        copy.start()
    for copy in copies:
        copy.wait()


def on_device(ny, nx, query_act, key_act, value_act, grad_gated, filter_taps, decay_rate):
    tokens, channels = query_act.shape
    rows_here, groups = filter_taps.shape
    whole = jax.ShapeDtypeStruct((tokens, channels), BF16)
    shapes = (whole, whole, whole, jax.ShapeDtypeStruct((rows_here, groups), F32))
    vmem = pl.BlockSpec(memory_space=pltpu.VMEM)
    hbm = pl.BlockSpec(memory_space=pl.ANY)
    dma = pltpu.SemaphoreType.DMA
    inner = pltpu.VMEM((tokens, channels), BF16)
    halo = pltpu.VMEM((2, L, channels), BF16)
    wide = pltpu.VMEM((CHUNKS, 2, LANES, 3 * L), BF16)
    by_device = pltpu.VMEM((2 * ny * nx, rows_here, L), F32)
    operands = (key_act, value_act, query_act, grad_gated, filter_taps, decay_rate.reshape(1, groups))
    operands = [pltpu.with_memory_space_constraint(x, pltpu.HBM) for x in operands]
    results = pl.pallas_call(
        functools.partial(kernel, ny, nx, rows_here),
        out_shape=shapes,
        in_specs=[hbm] * 6,
        out_specs=(vmem,) * 4,
        scratch_shapes=[
            inner, inner, inner, inner, halo, halo, wide, wide,
            pltpu.VMEM((CHUNKS, GROUPS, 2 * L, 2 * L), BF16),
            pltpu.VMEM((CHUNKS, GROUPS, L, L), F32),
            pltpu.VMEM((8 * GROUPS, L), F32),
            pltpu.VMEM((CHUNKS, GROUPS, L), F32),
            pltpu.VMEM((CHUNKS, GROUPS, L), F32),
            pltpu.VMEM((LANES, tokens), F32),
            pltpu.VMEM((LANES, tokens), F32),
            pltpu.VMEM((rows_here, groups), F32),
            pltpu.VMEM((1, groups), F32),
            pltpu.VMEM((ny, 2 * nx, rows_here, L), F32),
            by_device, by_device,
            pltpu.VMEM((L, L), F32),
            dma((6,)), dma((3, 2)), dma((3, 2)), dma((3, 2)), dma((3, 2)), dma((3,)), dma((3,)), pltpu.SemaphoreType.REGULAR((2,)),
        ],
        compiler_params=pltpu.CompilerParams(
            collective_id=0, has_side_effects=True, vmem_limit_bytes=VMEM_LIMIT
        ),
    )(*operands)
    return pl.pallas_call(
        write_out,
        out_shape=shapes,
        in_specs=[vmem] * 4,
        out_specs=(hbm,) * 4,
        scratch_shapes=[dma((4,))],
        compiler_params=pltpu.CompilerParams(vmem_limit_bytes=4 * 1024 * 1024),
    )(*results)


def solution(mesh):
    chips = mesh.shape["ctx"] // 2
    nx = 4 if chips >= 32 else 2
    return jax.shard_map(
        functools.partial(on_device, chips // nx, nx),
        mesh=mesh,
        in_specs=(P("ctx", "tp"),) * 5 + (P("tp"),),
        out_specs=(P("ctx", "tp"),) * 4,
        check_vma=False,
    )
```

```python
import functools

import jax
import jax.numpy as jnp
from jax import lax
from jax.experimental import pallas as pl
from jax.experimental.pallas import tpu as pltpu
from jax.sharding import PartitionSpec as P

L = 128
CH = 16
LANES = 128
CHUNKS = 4
GROUPS = LANES // CH
VMEM_LIMIT = 32 * 1024 * 1024
MESH = pl.DeviceIdType.MESH
F32, BF16 = jnp.float32, jnp.bfloat16


def dot(a, b, dims):
    return lax.dot_general(a, b, (dims, ((), ())), preferred_element_type=F32)


def flip(x):
    turn = 7 - lax.broadcasted_iota(jnp.int32, (8, LANES), 0)
    tiles = [jnp.take_along_axis(x[i : i + 8], turn, axis=0) for i in range(0, x.shape[0], 8)]
    return jnp.concatenate(tiles[::-1], axis=0)


def split_product(a, b, backward):
    whole = a.astype(F32) * b.astype(F32)
    whole = jnp.transpose(flip(whole) if backward else whole)
    high = whole.astype(BF16)
    return high, (whole - high.astype(F32)).astype(BF16)


def lanes(c):
    return pl.ds(pl.multiple_of(c * LANES, LANES), LANES)


def prepare(c, k, v, g, q, pt, st):
    for (a, b, out, backward) in ((k, v, pt, False), (g, q, st, True)):
        high, low = split_product(a[:, lanes(c)], b[:, lanes(c)], backward)
        out[c, 0, :, L:] = high
        out[c, 1, :, L:] = low


def prepare_halo(c, halo, out, backward, here):
    high, low = split_product(halo[0, :, lanes(c)], halo[1, :, lanes(c)], backward)
    keep = jnp.where(here, 1.0, 0.0).astype(BF16)
    out[c, 0, :, :L] = high * keep
    out[c, 1, :, :L] = low * keep


def diagonals(whole):
    return jnp.sum(pltpu.roll(whole, 0, 1, stride=1, stride_axis=0), axis=0, keepdims=True)


def lag_pairs(c, r, pt, st, before, after):
    rows = slice(CH * r, CH * r + CH)
    none = jnp.zeros((CH, L), BF16)
    p = [[pt[c, part, rows, L * b : L * b + L] for b in range(0 if before else 1, 3)] for part in (0, 1)]
    s = [[st[c, part, rows, L * b : L * b + L] for b in range(0 if after else 1, 3)] for part in (0, 1)]
    left = p[0] + p[1] + p[0]
    right = []
    for part in (0, 0, 1):
        last = s[part][0] if after else none
        if before:
            right.append(jnp.concatenate([none, s[part][-1]], axis=1))
        right.append(jnp.concatenate([s[part][-1], s[part][-2]], axis=1))
        right.append(jnp.concatenate([s[part][-2], last], axis=1))
    both = dot(jnp.concatenate(left, axis=0), jnp.concatenate(right, axis=0), ((0,), (0,)))
    row = lax.broadcasted_iota(jnp.int32, (L, L), 0)
    lane = lax.broadcasted_iota(jnp.int32, (L, L), 1)
    return jnp.where(lane + row < L, both[:, :L], both[:, L:])


def lag_inner(c, pt, st, diag):
    for r in range(GROUPS):
        diag[c % 2, r] = lag_pairs(c, r, pt, st, False, False)


def lag_whole(c, pt, st, before, lag):
    for r in range(GROUPS):
        lag[c, r : r + 1, :] = diagonals(lag_pairs(c, r, pt, st, before, not before))


def lag_cross(c, pt, st, pb, sb, diag, lag):
    row = lax.broadcasted_iota(jnp.int32, (L, L), 0)
    lane = lax.broadcasted_iota(jnp.int32, (L, L), 1)
    upper = lane + row < L
    none = jnp.zeros((CH, L), BF16)
    for r in range(0, GROUPS, 2):
        left, right = [], []
        for e in range(2):
            rows = slice(CH * (r + e), CH * (r + e) + CH)
            p = [pt[c, part, rows, pl.ds(pl.multiple_of(pb * L, L), L)] for part in (0, 1)]
            s = [st[c, part, rows, pl.ds(pl.multiple_of(sb * L, L), L)] for part in (0, 1)]
            for i, j in ((0, 0), (1, 0), (0, 1)):
                left.append(p[i])
                right.append(jnp.concatenate([s[j], none] if e == 0 else [none, s[j]], axis=1))
        both = dot(jnp.concatenate(left, axis=0), jnp.concatenate(right, axis=0), ((0,), (0,)))
        for e in range(2):
            whole = diag[c % 2, r + e] + jnp.where(upper, 0.0, both[:, L * e : L * e + L])
            lag[c, r + e : r + e + 1, :] = diagonals(whole)


def filter_matrix(line, upper):
    whole = pltpu.roll(jnp.broadcast_to(line, (L, L)), 0, 1, stride=1, stride_axis=0)
    high = whole.astype(BF16)
    low = (whole - high.astype(F32)).astype(BF16)
    now = jnp.concatenate([high * upper, low * upper], axis=1)
    return jnp.concatenate([jnp.concatenate([high, low], axis=1) - now, now], axis=0)


def convolve(c, pt, st, taps, mixed, back):
    row = lax.broadcasted_iota(jnp.int32, (L, L), 0)
    lane = lax.broadcasted_iota(jnp.int32, (L, L), 1)
    upper = jnp.where(lane >= row, 1.0, 0.0).astype(BF16)
    for r in range(GROUPS):
        rows = slice(CH * r, CH * r + CH)
        left = [x[c, part, rows, L * b : L * b + 2 * L] for x in (pt, st) for part in (0, 1) for b in (0, 1)]
        got = dot(jnp.concatenate(left, axis=0), filter_matrix(taps[c, r : r + 1, :], upper), ((1,), (0,)))
        for i, out in enumerate((mixed, back)):
            for b in (0, 1):
                high, low = CH * (4 * i + b), CH * (4 * i + 2 + b)
                out[rows, L * b : L * b + L] = (
                    got[high : high + CH, :L] + got[high : high + CH, L:] + got[low : low + CH, :L]
                )


def finish(c, k, v, g, mixed, back, gq, gk, gv):
    forward = jnp.transpose(mixed[...])
    backward = flip(jnp.transpose(back[...]))
    gq[:, lanes(c)] = (g[:, lanes(c)].astype(F32) * forward).astype(BF16)
    gk[:, lanes(c)] = (backward * v[:, lanes(c)].astype(F32)).astype(BF16)
    gv[:, lanes(c)] = (backward * k[:, lanes(c)].astype(F32)).astype(BF16)


def kernel(
    ny, nx, rows_here,
    k_hbm, v_hbm, q_hbm, g_hbm, taps_hbm, decay_hbm,
    gq, gk, gv, gf,
    k, v, q, g, kv_halo, qg_halo, pt, st, diag, taps, lag, mixed, back,
    taps_in, decay_in, gather, partial, reduced, all_taps,
    in_sem, kv_send, kv_recv, qg_send, qg_recv, send, recv, ready,
):
    n = ny * nx * 2
    me = lax.axis_index("ctx")
    chip, core = me // 2, me % 2
    nxt, prv = (me + 1) % n, (me + n - 1) % n
    tokens = 2 * L
    half = CHUNKS * LANES // 2
    groups = taps_hbm.shape[1]

    def hops(dy, dx):
        return min(dy, ny - dy) + min(dx, nx - dx)

    steps = [(dy, dx) for dy in range(ny) for dx in range(nx) if dy or dx]
    steps.sort(key=lambda step: -hops(*step))
    chips = [((chip // nx + dy) % ny) * nx + (chip % nx + dx) % nx for dy, dx in steps]
    everyone = [device for there in chips for device in (2 * there, 2 * there + 1)] + [me + 1 - 2 * core]

    loads = [
        pltpu.make_async_copy(src, dst, in_sem.at[i])
        for i, (src, dst) in enumerate(((k_hbm, k), (v_hbm, v), (g_hbm, g), (q_hbm, q)))
    ]

    def halo_copies(piece, lead, sources, first, dst, sends, recvs, there):
        columns = slice(lead + piece * LANES, lead + (piece + 1) * LANES) if piece < 2 else slice(half - lead, 2 * half - lead)
        return [
            pltpu.make_async_remote_copy(
                src_ref=src.at[first : first + L, columns], dst_ref=dst.at[i, :, columns],
                send_sem=sends.at[piece, i], recv_sem=recvs.at[piece, i],
                device_id={"ctx": there}, device_id_type=MESH,
            )
            for i, src in enumerate(sources)
        ]

    def kv_copies(piece):
        return halo_copies(piece, 0, (k, v), tokens - L, kv_halo, kv_send, kv_recv, nxt)

    def qg_copies(piece):
        return halo_copies(piece, half, (g, q), 0, qg_halo, qg_send, qg_recv, prv)

    def send_to(which, src, dst, there):
        return pltpu.make_async_remote_copy(
            src_ref=src, dst_ref=dst, send_sem=send.at[which], recv_sem=recv.at[which],
            device_id={"ctx": there}, device_id_type=MESH,
        )

    def bytes_of(which, slots):
        return send_to(which, slots, slots, nxt)

    def along_y(dy):
        return 2 * (((chip // nx + ny + dy) % ny) * nx + chip % nx) + core

    row = [2 * ((chip // nx) * nx + (chip % nx + dx) % nx) for dx in range(nx)]
    sorted_row = [row[dx] for dx in sorted(range(1, nx), key=lambda dx: -hops(0, dx))]

    def around(*distances):
        return sorted({d % ny for r in distances for d in (r, -r)} - {0})

    row_mates = [there + c for there in sorted_row for c in (0, 1)] + [me + 1 - 2 * core]
    near = [along_y(d) for d in around(2)] + row_mates[:2] + [nxt, prv] + [along_y(d) for d in around(1) if d not in around(2)] + row_mates[2:]
    barrier = pltpu.get_barrier_semaphore()
    for there in near:
        pl.semaphore_signal(barrier, inc=1, device_id={"ctx": there}, device_id_type=MESH)

    small = [
        pltpu.make_async_copy(taps_hbm, taps_in, in_sem.at[4]),
        pltpu.make_async_copy(decay_hbm, decay_in, in_sem.at[5]),
    ]
    for copy in small + loads:
        copy.start()

    for copy in small:
        copy.wait()
    mine = jnp.concatenate([taps_in[...], jnp.zeros((rows_here, L - groups), F32)], axis=1)
    place = me % (2 * nx)
    gather[pl.ds(chip // nx, 1), pl.ds(place, 1)] = mine[None, None]

    for copy in loads:
        copy.wait()
    def prepare_step(c, carry):
        prepare(c, k, v, g, q, pt, st)
        return carry

    lax.fori_loop(0, CHUNKS, prepare_step, 0)

    pl.semaphore_wait(barrier, len(near))
    def tell(which, *distances):
        for d in around(*distances):
            pl.semaphore_signal(ready.at[which], inc=1, device_id={"ctx": along_y(d)}, device_id_type=MESH)

    tell(0, 1, 2)
    my_row = gather.at[chip // nx]
    for there in row_mates:
        send_to(0, my_row.at[place], my_row.at[place], there).start()
    for piece in range(2):
        for copy in kv_copies(piece) + qg_copies(piece):
            copy.start()

    def inner_step(c, carry):
        lag_inner(c, pt, st, diag)
        return carry

    lax.fori_loop(2 * core, 2 * core + 2, inner_step, 0)
    for copy in kv_copies(2) + qg_copies(2):
        copy.start()
    pl.semaphore_wait(ready.at[0], len(around(1, 2)))
    tell(1, 2)

    def kv_arrived(piece, chunks):
        for copy in kv_copies(piece):
            copy.wait_recv()
        for c in chunks:
            prepare_halo(c, kv_halo, pt, False, me > 0)

    def qg_arrived(piece, chunks):
        for copy in qg_copies(piece):
            copy.wait_recv()
        for c in chunks:
            prepare_halo(c, qg_halo, st, True, me < n - 1)

    def cross_step(i, carry):
        c = (i + 2 - 2 * core) % CHUNKS
        h = c // 2
        for piece in range(2):

            @pl.when(c == piece)
            def _():
                kv_arrived(piece, [piece])

            @pl.when(c == 2 + piece)
            def _():
                qg_arrived(piece, [2 + piece])

        lag_cross(c, pt, st, 2 * h, 2 - 2 * h, diag, lag)
        return carry

    @pl.when(core == 0)
    def _():
        for piece in range(2):
            qg_arrived(piece, [2 + piece])

        def step(c, carry):
            lag_whole(c, pt, st, False, lag)
            return carry

        lax.fori_loop(2, 4, step, 0)

    @pl.when(core == 1)
    def _():
        for piece in range(2):
            kv_arrived(piece, [piece])

        def step(c, carry):
            lag_whole(c, pt, st, True, lag)
            return carry

        lax.fori_loop(0, 2, step, 0)


    bytes_of(0, my_row.at[: 2 * nx - 1]).wait_recv()
    for d in sorted(range(1, ny), key=lambda d: -hops(d, 0)):
        send_to(1, my_row, my_row, along_y(d)).start()

    lax.fori_loop(2, CHUNKS, cross_step, 0)

    per_lag = jnp.transpose(
        jnp.concatenate([lag[c] for c in range(CHUNKS)] + [jnp.zeros((L - CHUNKS * GROUPS, L), F32)], axis=0)
    )
    for i in range(n):
        partial[i] = per_lag[L - rows_here * (i + 1) : L - rows_here * i]
    reduced[pl.ds(me, 1)] = partial[pl.ds(me, 1)]
    pl.semaphore_wait(ready.at[1], len(around(2)))
    for there in everyone:
        send_to(2, partial.at[there], reduced.at[me], there).start()

    bytes_of(1, gather.at[: ny - 1]).wait_recv()
    for i in range(n):
        all_taps[rows_here * i : rows_here * (i + 1), :] = gather[i // (2 * nx), i % (2 * nx)]
    decay = jnp.concatenate([decay_in[...], jnp.zeros((1, L - groups), F32)], axis=1)
    step = lax.broadcasted_iota(jnp.int32, (L, L), 0).astype(F32)
    turned = jnp.transpose(all_taps[...] * jnp.exp(-decay * step))
    for c in range(CHUNKS):
        taps[c] = turned[GROUPS * c : GROUPS * c + GROUPS]

    def output_half(i):
        h = (i + core) % 2

        @pl.when(h == 0)
        def _():
            qg_arrived(2, [0, 1])

        @pl.when(h == 1)
        def _():
            kv_arrived(2, [2, 3])

        for j in range(2):
            convolve(2 * h + j, pt, st, taps, mixed.at[j], back.at[j])
            finish(2 * h + j, k, v, g, mixed.at[j], back.at[j], gq, gk, gv)

    output_half(0)
    output_half(1)

    bytes_of(2, reduced.at[: n - 1]).wait_recv()
    parts = [jnp.sum(reduced[i : i + n // 8], axis=0) for i in range(0, n, n // 8)]
    while len(parts) > 1:
        parts = [parts[i] + parts[i + 1] for i in range(0, len(parts), 2)]
    total = parts[0]
    total = jnp.concatenate([total[i : i + 1] for i in reversed(range(rows_here))], axis=0)
    lag_index = (me * rows_here + lax.broadcasted_iota(jnp.int32, (rows_here, L), 0)).astype(F32)
    gf[...] = (total * jnp.exp(-decay * lag_index) / float(tokens * n))[:, :groups]

    for piece in range(3):
        for copy in kv_copies(piece) + qg_copies(piece):
            copy.wait_send()
    bytes_of(0, my_row.at[: 2 * nx - 1]).wait_send()
    bytes_of(1, gather.at[: ny - 1]).wait_send()
    bytes_of(2, reduced.at[: n - 1]).wait_send()


def write_out(*refs):
    count = len(refs) // 2
    sems = refs[-1]
    copies = [pltpu.make_async_copy(refs[i], refs[count + i], sems.at[i]) for i in range(count)]
    for copy in copies:
        copy.start()
    for copy in copies:
        copy.wait()


def on_device(ny, nx, query_act, key_act, value_act, grad_gated, filter_taps, decay_rate):
    tokens, channels = query_act.shape
    rows_here, groups = filter_taps.shape
    whole = jax.ShapeDtypeStruct((tokens, channels), BF16)
    shapes = (whole, whole, whole, jax.ShapeDtypeStruct((rows_here, groups), F32))
    vmem = pl.BlockSpec(memory_space=pltpu.VMEM)
    hbm = pl.BlockSpec(memory_space=pl.ANY)
    dma = pltpu.SemaphoreType.DMA
    inner = pltpu.VMEM((tokens, channels), BF16)
    halo = pltpu.VMEM((2, L, channels), BF16)
    wide = pltpu.VMEM((CHUNKS, 2, LANES, 3 * L), BF16)
    by_device = pltpu.VMEM((2 * ny * nx, rows_here, L), F32)
    operands = (key_act, value_act, query_act, grad_gated, filter_taps, decay_rate.reshape(1, groups))
    operands = [pltpu.with_memory_space_constraint(x, pltpu.HBM) for x in operands]
    results = pl.pallas_call(
        functools.partial(kernel, ny, nx, rows_here),
        out_shape=shapes,
        in_specs=[hbm] * 6,
        out_specs=(vmem,) * 4,
        scratch_shapes=[
            inner, inner, inner, inner, halo, halo, wide, wide,
            pltpu.VMEM((2, GROUPS, L, L), F32),
            pltpu.VMEM((CHUNKS, GROUPS, L), F32),
            pltpu.VMEM((CHUNKS, GROUPS, L), F32),
            pltpu.VMEM((2, LANES, tokens), F32),
            pltpu.VMEM((2, LANES, tokens), F32),
            pltpu.VMEM((rows_here, groups), F32),
            pltpu.VMEM((1, groups), F32),
            pltpu.VMEM((ny, 2 * nx, rows_here, L), F32),
            by_device, by_device,
            pltpu.VMEM((L, L), F32),
            dma((6,)), dma((3, 2)), dma((3, 2)), dma((3, 2)), dma((3, 2)), dma((3,)), dma((3,)), pltpu.SemaphoreType.REGULAR((2,)),
        ],
        compiler_params=pltpu.CompilerParams(
            collective_id=0, has_side_effects=True, vmem_limit_bytes=VMEM_LIMIT
        ),
    )(*operands)
    return pl.pallas_call(
        write_out,
        out_shape=shapes,
        in_specs=[vmem] * 4,
        out_specs=(hbm,) * 4,
        scratch_shapes=[dma((4,))],
        compiler_params=pltpu.CompilerParams(vmem_limit_bytes=4 * 1024 * 1024),
    )(*results)


def solution(mesh):
    chips = mesh.shape["ctx"] // 2
    nx = 4 if chips >= 32 else 2
    return jax.shard_map(
        functools.partial(on_device, chips // nx, nx),
        mesh=mesh,
        in_specs=(P("ctx", "tp"),) * 5 + (P("tp"),),
        out_specs=(P("ctx", "tp"),) * 4,
        check_vma=False,
    )
```

```python
import functools

import jax
import jax.numpy as jnp
from jax import lax
from jax.experimental import pallas as pl
from jax.experimental.pallas import tpu as pltpu
from jax.sharding import PartitionSpec as P

L = 128
CH = 16
LANES = 128
CHUNKS = 4
GROUPS = LANES // CH
VMEM_LIMIT = 32 * 1024 * 1024
MESH = pl.DeviceIdType.MESH
F32, BF16 = jnp.float32, jnp.bfloat16


def dot(a, b, dims):
    return lax.dot_general(a, b, (dims, ((), ())), preferred_element_type=F32)


def flip(x):
    turn = 7 - lax.broadcasted_iota(jnp.int32, (8, LANES), 0)
    tiles = [jnp.take_along_axis(x[i : i + 8], turn, axis=0) for i in range(0, x.shape[0], 8)]
    return jnp.concatenate(tiles[::-1], axis=0)


def split_product(a, b, backward):
    whole = a.astype(F32) * b.astype(F32)
    whole = jnp.transpose(flip(whole) if backward else whole)
    high = whole.astype(BF16)
    return high, (whole - high.astype(F32)).astype(BF16)


def lanes(c):
    return pl.ds(pl.multiple_of(c * LANES, LANES), LANES)


def prepare(c, k, v, g, q, pt, st):
    for (a, b, out, backward) in ((k, v, pt, False), (g, q, st, True)):
        high, low = split_product(a[:, lanes(c)], b[:, lanes(c)], backward)
        out[c, 0, :, L:] = high
        out[c, 1, :, L:] = low


def prepare_halo(c, halo, out, backward, here):
    high, low = split_product(halo[0, :, lanes(c)], halo[1, :, lanes(c)], backward)
    keep = jnp.where(here, 1.0, 0.0).astype(BF16)
    out[c, 0, :, :L] = high * keep
    out[c, 1, :, :L] = low * keep


def diagonals(whole):
    return jnp.sum(pltpu.roll(whole, 0, 1, stride=1, stride_axis=0), axis=0, keepdims=True)


def lag_pairs(c, r, pt, st, before, after):
    rows = slice(CH * r, CH * r + CH)
    none = jnp.zeros((CH, L), BF16)
    p = [[pt[c, part, rows, L * b : L * b + L] for b in range(0 if before else 1, 3)] for part in (0, 1)]
    s = [[st[c, part, rows, L * b : L * b + L] for b in range(0 if after else 1, 3)] for part in (0, 1)]
    left = p[0] + p[1] + p[0]
    right = []
    for part in (0, 0, 1):
        last = s[part][0] if after else none
        if before:
            right.append(jnp.concatenate([none, s[part][-1]], axis=1))
        right.append(jnp.concatenate([s[part][-1], s[part][-2]], axis=1))
        right.append(jnp.concatenate([s[part][-2], last], axis=1))
    both = dot(jnp.concatenate(left, axis=0), jnp.concatenate(right, axis=0), ((0,), (0,)))
    row = lax.broadcasted_iota(jnp.int32, (L, L), 0)
    lane = lax.broadcasted_iota(jnp.int32, (L, L), 1)
    return jnp.where(lane + row < L, both[:, :L], both[:, L:])


def lag_inner(c, pt, st, diag):
    for r in range(GROUPS):
        diag[c % 2, r] = lag_pairs(c, r, pt, st, False, False)


def lag_whole(c, pt, st, before, lag):
    for r in range(GROUPS):
        lag[c, r : r + 1, :] = diagonals(lag_pairs(c, r, pt, st, before, not before))


def lag_cross(c, pt, st, pb, sb, diag, lag):
    row = lax.broadcasted_iota(jnp.int32, (L, L), 0)
    lane = lax.broadcasted_iota(jnp.int32, (L, L), 1)
    upper = lane + row < L
    none = jnp.zeros((CH, L), BF16)
    for r in range(0, GROUPS, 2):
        left, right = [], []
        for e in range(2):
            rows = slice(CH * (r + e), CH * (r + e) + CH)
            p = [pt[c, part, rows, pl.ds(pl.multiple_of(pb * L, L), L)] for part in (0, 1)]
            s = [st[c, part, rows, pl.ds(pl.multiple_of(sb * L, L), L)] for part in (0, 1)]
            for i, j in ((0, 0), (1, 0), (0, 1)):
                left.append(p[i])
                right.append(jnp.concatenate([s[j], none] if e == 0 else [none, s[j]], axis=1))
        both = dot(jnp.concatenate(left, axis=0), jnp.concatenate(right, axis=0), ((0,), (0,)))
        for e in range(2):
            whole = diag[c % 2, r + e] + jnp.where(upper, 0.0, both[:, L * e : L * e + L])
            lag[c, r + e : r + e + 1, :] = diagonals(whole)


def filter_matrix(line, upper):
    whole = pltpu.roll(jnp.broadcast_to(line, (L, L)), 0, 1, stride=1, stride_axis=0)
    high = whole.astype(BF16)
    low = (whole - high.astype(F32)).astype(BF16)
    now = jnp.concatenate([high * upper, low * upper], axis=1)
    return jnp.concatenate([jnp.concatenate([high, low], axis=1) - now, now], axis=0)


def convolve(c, pt, st, taps, mixed, back):
    row = lax.broadcasted_iota(jnp.int32, (L, L), 0)
    lane = lax.broadcasted_iota(jnp.int32, (L, L), 1)
    upper = jnp.where(lane >= row, 1.0, 0.0).astype(BF16)
    for r in range(GROUPS):
        rows = slice(CH * r, CH * r + CH)
        left = [x[c, part, rows, L * b : L * b + 2 * L] for x in (pt, st) for part in (0, 1) for b in (0, 1)]
        got = dot(jnp.concatenate(left, axis=0), filter_matrix(taps[c, r : r + 1, :], upper), ((1,), (0,)))
        for i, out in enumerate((mixed, back)):
            for b in (0, 1):
                high, low = CH * (4 * i + b), CH * (4 * i + 2 + b)
                out[rows, L * b : L * b + L] = (
                    got[high : high + CH, :L] + got[high : high + CH, L:] + got[low : low + CH, :L]
                )


def finish(c, k, v, g, mixed, back, gq, gk, gv):
    forward = jnp.transpose(mixed[...])
    backward = flip(jnp.transpose(back[...]))
    gq[:, lanes(c)] = (g[:, lanes(c)].astype(F32) * forward).astype(BF16)
    gk[:, lanes(c)] = (backward * v[:, lanes(c)].astype(F32)).astype(BF16)
    gv[:, lanes(c)] = (backward * k[:, lanes(c)].astype(F32)).astype(BF16)


def kernel(
    ny, nx, rows_here,
    k_hbm, v_hbm, q_hbm, g_hbm, taps_hbm, decay_hbm,
    gq, gk, gv, gf,
    k, v, q, g, kv_halo, qg_halo, pt, st, diag, taps, lag, mixed, back,
    taps_in, decay_in, gather, partial, reduced, all_taps,
    in_sem, kv_send, kv_recv, qg_send, qg_recv, send, recv, ready,
):
    n = ny * nx * 2
    me = lax.axis_index("ctx")
    chip, core = me // 2, me % 2
    nxt, prv = (me + 1) % n, (me + n - 1) % n
    tokens = 2 * L
    half = CHUNKS * LANES // 2
    groups = taps_hbm.shape[1]

    def hops(dy, dx):
        return min(dy, ny - dy) + min(dx, nx - dx)

    steps = [(dy, dx) for dy in range(ny) for dx in range(nx) if dy or dx]
    steps.sort(key=lambda step: -hops(*step))
    chips = [((chip // nx + dy) % ny) * nx + (chip % nx + dx) % nx for dy, dx in steps]
    everyone = [device for there in chips for device in (2 * there, 2 * there + 1)] + [me + 1 - 2 * core]

    loads = [
        pltpu.make_async_copy(src, dst, in_sem.at[i])
        for i, (src, dst) in enumerate(((k_hbm, k), (v_hbm, v), (g_hbm, g), (q_hbm, q)))
    ]

    def halo_copies(piece, lead, sources, first, dst, sends, recvs, there):
        columns = slice(lead + piece * LANES, lead + (piece + 1) * LANES) if piece < 2 else slice(half - lead, 2 * half - lead)
        return [
            pltpu.make_async_remote_copy(
                src_ref=src.at[first : first + L, columns], dst_ref=dst.at[i, :, columns],
                send_sem=sends.at[piece, i], recv_sem=recvs.at[piece, i],
                device_id={"ctx": there}, device_id_type=MESH,
            )
            for i, src in enumerate(sources)
        ]

    def kv_copies(piece):
        return halo_copies(piece, 0, (k, v), tokens - L, kv_halo, kv_send, kv_recv, nxt)

    def qg_copies(piece):
        return halo_copies(piece, half, (g, q), 0, qg_halo, qg_send, qg_recv, prv)

    def send_to(which, src, dst, there):
        return pltpu.make_async_remote_copy(
            src_ref=src, dst_ref=dst, send_sem=send.at[which], recv_sem=recv.at[which],
            device_id={"ctx": there}, device_id_type=MESH,
        )

    def bytes_of(which, slots):
        return send_to(which, slots, slots, nxt)

    def along_y(dy):
        return 2 * (((chip // nx + ny + dy) % ny) * nx + chip % nx) + core

    row = [2 * ((chip // nx) * nx + (chip % nx + dx) % nx) for dx in range(nx)]
    sorted_row = [row[dx] for dx in sorted(range(1, nx), key=lambda dx: -hops(0, dx))]

    def around(*distances):
        return sorted({d % ny for r in distances for d in (r, -r)} - {0})

    row_mates = [there + c for there in sorted_row for c in (0, 1)] + [me + 1 - 2 * core]
    near = [along_y(d) for d in around(2)] + row_mates[:2] + [nxt, prv] + [along_y(d) for d in around(1) if d not in around(2)] + row_mates[2:]
    barrier = pltpu.get_barrier_semaphore()
    for there in near:
        pl.semaphore_signal(barrier, inc=1, device_id={"ctx": there}, device_id_type=MESH)

    small = [
        pltpu.make_async_copy(taps_hbm, taps_in, in_sem.at[4]),
        pltpu.make_async_copy(decay_hbm, decay_in, in_sem.at[5]),
    ]
    for copy in small + loads:
        copy.start()

    for copy in small:
        copy.wait()
    mine = jnp.concatenate([taps_in[...], jnp.zeros((rows_here, L - groups), F32)], axis=1)
    place = me % (2 * nx)
    gather[pl.ds(chip // nx, 1), pl.ds(place, 1)] = mine[None, None]

    pl.semaphore_wait(barrier, len(near))
    def tell(which, *distances):
        for d in around(*distances):
            pl.semaphore_signal(ready.at[which], inc=1, device_id={"ctx": along_y(d)}, device_id_type=MESH)

    tell(0, 1, 2)
    my_row = gather.at[chip // nx]
    for there in row_mates:
        send_to(0, my_row.at[place], my_row.at[place], there).start()
    for copy in loads:
        copy.wait()
    for piece in range(2):
        for copy in kv_copies(piece) + qg_copies(piece):
            copy.start()
    def prepare_step(c, carry):
        prepare(c, k, v, g, q, pt, st)
        return carry

    lax.fori_loop(0, CHUNKS, prepare_step, 0)


    def inner_step(c, carry):
        lag_inner(c, pt, st, diag)
        return carry

    lax.fori_loop(2 * core, 2 * core + 2, inner_step, 0)
    for copy in kv_copies(2) + qg_copies(2):
        copy.start()
    pl.semaphore_wait(ready.at[0], len(around(1, 2)))
    tell(1, 2)

    def kv_arrived(piece, chunks):
        for copy in kv_copies(piece):
            copy.wait_recv()
        for c in chunks:
            prepare_halo(c, kv_halo, pt, False, me > 0)

    def qg_arrived(piece, chunks):
        for copy in qg_copies(piece):
            copy.wait_recv()
        for c in chunks:
            prepare_halo(c, qg_halo, st, True, me < n - 1)

    def cross_step(i, carry):
        c = (i + 2 - 2 * core) % CHUNKS
        h = c // 2
        for piece in range(2):

            @pl.when(c == piece)
            def _():
                kv_arrived(piece, [piece])

            @pl.when(c == 2 + piece)
            def _():
                qg_arrived(piece, [2 + piece])

        lag_cross(c, pt, st, 2 * h, 2 - 2 * h, diag, lag)
        return carry

    @pl.when(core == 0)
    def _():
        for piece in range(2):
            qg_arrived(piece, [2 + piece])

        def step(c, carry):
            lag_whole(c, pt, st, False, lag)
            return carry

        lax.fori_loop(2, 4, step, 0)

    @pl.when(core == 1)
    def _():
        for piece in range(2):
            kv_arrived(piece, [piece])

        def step(c, carry):
            lag_whole(c, pt, st, True, lag)
            return carry

        lax.fori_loop(0, 2, step, 0)


    bytes_of(0, my_row.at[: 2 * nx - 1]).wait_recv()
    for d in sorted(range(1, ny), key=lambda d: -hops(d, 0)):
        send_to(1, my_row, my_row, along_y(d)).start()

    lax.fori_loop(2, CHUNKS, cross_step, 0)

    per_lag = jnp.transpose(
        jnp.concatenate([lag[c] for c in range(CHUNKS)] + [jnp.zeros((L - CHUNKS * GROUPS, L), F32)], axis=0)
    )
    for i in range(n):
        partial[i] = per_lag[L - rows_here * (i + 1) : L - rows_here * i]
    reduced[pl.ds(me, 1)] = partial[pl.ds(me, 1)]
    pl.semaphore_wait(ready.at[1], len(around(2)))
    for there in everyone:
        send_to(2, partial.at[there], reduced.at[me], there).start()

    bytes_of(1, gather.at[: ny - 1]).wait_recv()
    for i in range(n):
        all_taps[rows_here * i : rows_here * (i + 1), :] = gather[i // (2 * nx), i % (2 * nx)]
    decay = jnp.concatenate([decay_in[...], jnp.zeros((1, L - groups), F32)], axis=1)
    step = lax.broadcasted_iota(jnp.int32, (L, L), 0).astype(F32)
    turned = jnp.transpose(all_taps[...] * jnp.exp(-decay * step))
    for c in range(CHUNKS):
        taps[c] = turned[GROUPS * c : GROUPS * c + GROUPS]

    def output_half(i):
        h = (i + core) % 2

        @pl.when(h == 0)
        def _():
            qg_arrived(2, [0, 1])

        @pl.when(h == 1)
        def _():
            kv_arrived(2, [2, 3])

        for j in range(2):
            convolve(2 * h + j, pt, st, taps, mixed.at[j], back.at[j])
            finish(2 * h + j, k, v, g, mixed.at[j], back.at[j], gq, gk, gv)

    output_half(0)
    output_half(1)

    bytes_of(2, reduced.at[: n - 1]).wait_recv()
    parts = [jnp.sum(reduced[i : i + n // 8], axis=0) for i in range(0, n, n // 8)]
    while len(parts) > 1:
        parts = [parts[i] + parts[i + 1] for i in range(0, len(parts), 2)]
    total = parts[0]
    total = jnp.concatenate([total[i : i + 1] for i in reversed(range(rows_here))], axis=0)
    lag_index = (me * rows_here + lax.broadcasted_iota(jnp.int32, (rows_here, L), 0)).astype(F32)
    gf[...] = (total * jnp.exp(-decay * lag_index) / float(tokens * n))[:, :groups]

    for piece in range(3):
        for copy in kv_copies(piece) + qg_copies(piece):
            copy.wait_send()
    bytes_of(0, my_row.at[: 2 * nx - 1]).wait_send()
    bytes_of(1, gather.at[: ny - 1]).wait_send()
    bytes_of(2, reduced.at[: n - 1]).wait_send()


def write_out(*refs):
    count = len(refs) // 2
    sems = refs[-1]
    copies = [pltpu.make_async_copy(refs[i], refs[count + i], sems.at[i]) for i in range(count)]
    for copy in copies:
        copy.start()
    for copy in copies:
        copy.wait()


def on_device(ny, nx, query_act, key_act, value_act, grad_gated, filter_taps, decay_rate):
    tokens, channels = query_act.shape
    rows_here, groups = filter_taps.shape
    whole = jax.ShapeDtypeStruct((tokens, channels), BF16)
    shapes = (whole, whole, whole, jax.ShapeDtypeStruct((rows_here, groups), F32))
    vmem = pl.BlockSpec(memory_space=pltpu.VMEM)
    hbm = pl.BlockSpec(memory_space=pl.ANY)
    dma = pltpu.SemaphoreType.DMA
    inner = pltpu.VMEM((tokens, channels), BF16)
    halo = pltpu.VMEM((2, L, channels), BF16)
    wide = pltpu.VMEM((CHUNKS, 2, LANES, 3 * L), BF16)
    by_device = pltpu.VMEM((2 * ny * nx, rows_here, L), F32)
    operands = (key_act, value_act, query_act, grad_gated, filter_taps, decay_rate.reshape(1, groups))
    operands = [pltpu.with_memory_space_constraint(x, pltpu.HBM) for x in operands]
    results = pl.pallas_call(
        functools.partial(kernel, ny, nx, rows_here),
        out_shape=shapes,
        in_specs=[hbm] * 6,
        out_specs=(vmem,) * 4,
        scratch_shapes=[
            inner, inner, inner, inner, halo, halo, wide, wide,
            pltpu.VMEM((2, GROUPS, L, L), F32),
            pltpu.VMEM((CHUNKS, GROUPS, L), F32),
            pltpu.VMEM((CHUNKS, GROUPS, L), F32),
            pltpu.VMEM((2, LANES, tokens), F32),
            pltpu.VMEM((2, LANES, tokens), F32),
            pltpu.VMEM((rows_here, groups), F32),
            pltpu.VMEM((1, groups), F32),
            pltpu.VMEM((ny, 2 * nx, rows_here, L), F32),
            by_device, by_device,
            pltpu.VMEM((L, L), F32),
            dma((6,)), dma((3, 2)), dma((3, 2)), dma((3, 2)), dma((3, 2)), dma((3,)), dma((3,)), pltpu.SemaphoreType.REGULAR((2,)),
        ],
        compiler_params=pltpu.CompilerParams(
            collective_id=0, has_side_effects=True, vmem_limit_bytes=VMEM_LIMIT
        ),
    )(*operands)
    return pl.pallas_call(
        write_out,
        out_shape=shapes,
        in_specs=[vmem] * 4,
        out_specs=(hbm,) * 4,
        scratch_shapes=[dma((4,))],
        compiler_params=pltpu.CompilerParams(vmem_limit_bytes=4 * 1024 * 1024),
    )(*results)


def solution(mesh):
    chips = mesh.shape["ctx"] // 2
    nx = 4 if chips >= 32 else 2
    return jax.shard_map(
        functools.partial(on_device, chips // nx, nx),
        mesh=mesh,
        in_specs=(P("ctx", "tp"),) * 5 + (P("tp"),),
        out_specs=(P("ctx", "tp"),) * 4,
        check_vma=False,
    )
```
